32 devices in a mesh: league: 2 (over y), snap: 4 (over z), tp: 4 (over x, core).
Axes of the slice: x: 2, y: 2, z: 4, core: 2. Of those that a mesh axis runs over, the one named last changes fastest.
Arguments:
- block_states: bfloat16 [8, 128, 4096], P(('league', 'snap'), None, 'tp'), parts along dimension 0, may hold values from -6 to 6
- lengths: int32 [8], P('league'), parts along dimension 0, may hold values from 1 to 128, as said below
- norm_gain: float32 [4, 4096], P('snap'), may hold values from 0.5 to 2
- query_weight: bfloat16 [4, 4096, 4096], P('snap', None, 'tp'), may hold values from -4 to 4
- keyval_weight: bfloat16 [4, 4096, 512], P('snap', 'tp'), may hold values from -0.09375 to 0.09375
Outputs:
- ensemble_out: bfloat16 [8, 128, 4096], P(('league', 'snap'), None, 'tp'), parts along dimension 0
The draws below stay inside these ranges and needn't reach their ends.
There are 2 independent parts, one for each index of `league`. The reference program is written for one: setup_inputs(seed, part) draws one part's arguments, and reference() takes and returns one part's arrays. A program takes and returns all parts, laid end to end along the dimension named above; an argument that names none is the same for every part. Nothing has to cross between parts.
Inputs may be any that keep to these rules, and one draw needn't show every extreme that they name: `lengths`: some block has exactly 128 valid tokens.
All inputs are finite; a program needn't handle non-finite values.
Results may differ from the reference program's by a relative error of at most 0.008.
The reference program's roundings to bfloat16 on the way (of `normed`, `queries`, `keyval`, `key_heads`, `probabilities` and `context`) count: a program that leaves them out, or rounds other values in their place, can miss the bound.
Values may be sent and summed in bfloat16 or wider, within the bound.
No kernel may reach another device: no remote copies, remote signals or barrier semaphores. Data moves between devices by JAX's collectives and lax.ppermute only.
A program may use at most 64 MiB of HBM per device.

```python
import math
import jax
import jax.numpy as jnp
from jax import lax

D = 4096
QHEADS = 64
KVHEADS = 4
HD = 64
ROWS = 128
VISITS = 4
SNAPSHOTS = 4
BLOCKS = 4


def draw_lengths(key, part):
    key = jax.random.fold_in(key, 11)
    first_key, second_key = jax.random.split(key)
    drawn = jax.random.randint(first_key, (BLOCKS,), 1, ROWS + 1, dtype=jnp.int32)
    chosen = jax.random.randint(second_key, (), 0, BLOCKS, dtype=jnp.int32)
    return jnp.where(jnp.arange(BLOCKS, dtype=jnp.int32) == chosen, ROWS, drawn).astype(jnp.int32)


def draw_query_weight(key, part):
    key = jax.random.fold_in(key, 23)
    entry_key = jax.random.fold_in(key, 0)
    entries = jax.random.truncated_normal(entry_key, -4.0, 4.0, (SNAPSHOTS, D, QHEADS, HD), jnp.float32) * D ** (-0.5)
    return entries.reshape(SNAPSHOTS, D, QHEADS * HD).astype(jnp.bfloat16)


def levels(stream_key, shape, cuts, least, high):
    level = 1.0
    for axis_at, parts in cuts:
        heights = jax.random.uniform(jax.random.fold_in(jax.random.fold_in(stream_key, 6), axis_at), (parts,), jnp.float32, least / len(cuts), high / len(cuts))
        level = level * jnp.repeat(jnp.exp(heights), shape[axis_at] // parts).reshape((-1,) + (1,) * (len(shape) - 1 - axis_at))
    return level


def scatter_about(key, extent, width, reach, cuts=(), held_as=jnp.bfloat16):
    result = jax.random.normal(key, extent, jnp.float32) * width
    if len(cuts) > 0:
        result = levels(key, extent, cuts, -0.22, 0.18) * result
    return jnp.clip(result, min=-reach, max=reach).astype(held_as)


def setup_inputs(seed: int = 0, part: int = 0) -> dict:
    arg_keys = jax.random.split(jax.random.key(seed), 6)
    part_splits = jax.random.split(jax.random.fold_in(arg_keys[5], part), 6)
    block_states = scatter_about(part_splits[0], (BLOCKS, ROWS, D), 1.0, 6.0, ((0, 4), (2, 4)))
    lengths = draw_lengths(jax.random.fold_in(jax.random.fold_in(arg_keys[5], part), 71), part)
    norm_gain = jnp.clip(jnp.exp(math.log(2.0) - 1.3862944 * jax.random.uniform(arg_keys[2], (SNAPSHOTS, D), jnp.float32) ** levels(arg_keys[2], (SNAPSHOTS, D), ((0, 4),), -0.2, 0.2)), 0.5, 2.0)
    query_weight = draw_query_weight(jax.random.fold_in(arg_keys[5], 71), part)
    keyval_weight = scatter_about(arg_keys[4], (SNAPSHOTS, D, 2 * KVHEADS * HD), D ** -0.5, 0.09375, ((0, 4), (1, 4)))
    return {"block_states": block_states, "lengths": lengths, "norm_gain": norm_gain, "query_weight": query_weight, "keyval_weight": keyval_weight}


EPSILON = 1e-05
ROPE_BASE = 500000.0

def rope_tables(row_count, head_width):
    half_width = head_width // 2
    positions = jnp.arange(row_count, dtype=jnp.float32)[:, None]
    frequency = ROPE_BASE ** (-jnp.arange(half_width, dtype=jnp.float32) * 2.0 / head_width)
    angles = positions * frequency[None, :]
    return (jnp.cos(angles), jnp.sin(angles))

def rotate(head_vectors, cosine_table, sine_table):
    half_width = head_vectors.shape[-1] // 2
    first_half = head_vectors[..., :half_width]
    second_half = head_vectors[..., half_width:]
    cosine_part = cosine_table[:, None, :]
    sine_part = sine_table[:, None, :]
    return jnp.concatenate([first_half * cosine_part - second_half * sine_part, first_half * sine_part + second_half * cosine_part], axis=-1)

def snapshot_term(states, length, gain_row, query_proj, keyval_proj):
    row_count = states.shape[0]
    states_f32 = states.astype(jnp.float32)
    normed = (states_f32 * lax.rsqrt(lax.optimization_barrier(jnp.mean(states_f32 * states_f32, axis=1, keepdims=True)) + EPSILON) * gain_row[None, :]).astype(jnp.bfloat16)
    cosine_table, sine_table = rope_tables(row_count, HD)
    queries = jnp.dot(normed, query_proj, preferred_element_type=jnp.float32)
    queries = rotate(queries.reshape(row_count, QHEADS, HD), cosine_table, sine_table).astype(jnp.bfloat16)
    keyval = jnp.dot(normed, keyval_proj, preferred_element_type=jnp.float32).astype(jnp.bfloat16)
    keyval = keyval.reshape(row_count, KVHEADS, 2, HD)
    key_heads = rotate(keyval[:, :, 0].astype(jnp.float32), cosine_table, sine_table).astype(jnp.bfloat16)
    value_heads = keyval[:, :, 1]
    group_size = QHEADS // KVHEADS
    key_full = jnp.repeat(key_heads, group_size, axis=1)
    value_full = jnp.repeat(value_heads, group_size, axis=1)
    scores = jnp.einsum('qhd,khd->hqk', queries.astype(jnp.float32), key_full.astype(jnp.float32)) * HD ** (-0.5)
    positions = jnp.arange(row_count, dtype=jnp.int32)
    allowed = (positions[None, :] <= positions[:, None]) & (positions[None, :] < length)
    masked = jnp.where(allowed[None], scores, jnp.float32(-1e+30))
    row_top = lax.optimization_barrier(jnp.max(masked, axis=2, keepdims=True))
    weights = jnp.where(allowed[None], jnp.exp(masked - row_top), 0.0)
    probabilities = (weights / lax.optimization_barrier(jnp.sum(weights, axis=2, keepdims=True))).astype(jnp.bfloat16)
    context = jnp.einsum('hqk,khd->qhd', probabilities.astype(jnp.float32), value_full.astype(jnp.float32)).astype(jnp.bfloat16)
    return context.reshape(row_count, QHEADS * HD).astype(jnp.float32)

def reference(block_states, lengths, norm_gain, query_weight, keyval_weight):

    def one_block(block_index):
        states = block_states[block_index]
        length = lengths[block_index]
        total_sum = jnp.zeros((ROWS, QHEADS * HD), jnp.float32)
        for visit_step in range(VISITS):
            snapshot = (block_index + visit_step) % SNAPSHOTS
            total_sum = total_sum + snapshot_term(states, length, norm_gain[snapshot], query_weight[snapshot], keyval_weight[snapshot])
        row_keep = (jnp.arange(ROWS, dtype=jnp.int32) < length)[:, None]
        return jnp.where(row_keep, total_sum / VISITS, 0.0).astype(jnp.bfloat16)
    return lax.map(one_block, jnp.arange(BLOCKS, dtype=jnp.int32))
```

```python
import functools

import jax
import jax.numpy as jnp
from jax import lax
from jax.experimental import pallas as pl
from jax.experimental.pallas import tpu as pltpu
from jax.sharding import PartitionSpec as P

QHEADS = 64
KVHEADS = 4
HD = 64
VISITS = 4
LANES = 128

EPSILON = 1e-05
ROPE_BASE = 500000.0
LOG2E = 1.4426950408889634


def ring_pairs(count, by):
    return [(i, (i + by) % count) for i in range(count)]


def swapped(array, with_bits):
    count = lax.axis_size("tp")
    return lax.ppermute(array, "tp", [(i, i ^ with_bits) for i in range(count)])


def rope_tables(row_count):
    half = HD // 2
    positions = jnp.arange(row_count, dtype=jnp.float32)[:, None]
    frequency = ROPE_BASE ** (-jnp.arange(half, dtype=jnp.float32) * 2.0 / HD)
    angles = positions * frequency[None, :]
    cosine, sine = jnp.cos(angles), jnp.sin(angles)
    repeats = LANES // HD
    return (
        jnp.concatenate([cosine, cosine] * repeats, axis=1),
        jnp.concatenate([-sine, sine] * repeats, axis=1),
    )


def rotated(pair, cosine, signed_sine, in_first_half):
    half = HD // 2
    partner = jnp.where(
        in_first_half, pltpu.roll(pair, LANES - half, 1), pltpu.roll(pair, half, 1)
    )
    return pair * cosine + partner * signed_sine


def visit_kernel(parts, visit, lengths_ref, *refs):
    shards = refs[:parts]
    gain_ref, query_ref = refs[parts : parts + 2]
    keyvals = refs[parts + 2 : 2 * parts + 2]
    cosine_ref, sine_ref, out_ref, normed_ref, query_out_ref = refs[2 * parts + 2 :]
    rows, features = shards[0].shape
    width = parts * features
    rank = lax.axis_index("tp")
    snaps = lax.axis_size("snap")
    block = lax.rem(lax.axis_index("snap") + (snaps - visit), snaps)
    length = lengths_ref[block]

    squares = jnp.zeros((rows, 1), jnp.float32)
    for shard in shards:
        values = shard[...].astype(jnp.float32)
        squares += jnp.sum(values * values, axis=1, keepdims=True)
    scale = lax.rsqrt(squares / width + EPSILON)
    keyval = jnp.zeros((rows, keyvals[0].shape[1]), jnp.float32)
    for bits, shard in enumerate(shards):
        owner = lax.bitwise_xor(rank, jnp.int32(bits))
        normed = (shard[...].astype(jnp.float32) * scale * gain_ref[pl.ds(owner, 1), :]).astype(
            jnp.bfloat16
        )
        normed_ref[owner] = normed
        keyval += jnp.dot(normed, keyvals[bits][...], preferred_element_type=jnp.float32)

    cosine, sine = cosine_ref[...], sine_ref[...]
    lane = lax.broadcasted_iota(jnp.int32, (rows, LANES), 1)
    in_first_half = lax.rem(lane, HD) < HD // 2
    in_first_head = lane < HD
    keyval = keyval.astype(jnp.bfloat16).astype(jnp.float32)
    keys = jnp.where(in_first_head, rotated(keyval, cosine, sine, in_first_half), 0.0)
    keys = jnp.concatenate([keys, pltpu.roll(keys, HD, 1)], axis=0).astype(jnp.bfloat16)
    values = jnp.where(in_first_head, 0.0, keyval)
    values = jnp.concatenate([pltpu.roll(values, HD, 1), values], axis=0).astype(jnp.bfloat16)

    row = lax.broadcasted_iota(jnp.int32, (rows, rows), 0)
    column = lax.broadcasted_iota(jnp.int32, (rows, rows), 1)
    allowed = (column <= row) & (column < length)
    step = 2 * LANES
    for start in range(0, query_ref.shape[2], step):
        total = jnp.zeros((rows, step), jnp.float32)
        for part in range(parts):
            total += jnp.dot(
                normed_ref[part],
                query_ref[part, :, start : start + step],
                preferred_element_type=jnp.float32,
            )
        for pair in range(0, step, LANES):
            queries = rotated(
                total[:, pair : pair + LANES], cosine, sine, in_first_half
            ).astype(jnp.bfloat16)
            scores = lax.dot_general(
                queries, keys, (((1,), (1,)), ((), ())), preferred_element_type=jnp.float32
            )
            halves = []
            for head in range(2):
                mine = jnp.where(allowed, scores[:, head * rows : (head + 1) * rows], -1e30)
                top = jnp.max(mine, axis=1, keepdims=True)
                weights = jnp.exp2((mine - top) * (LOG2E * HD**-0.5))
                whole = jnp.sum(weights, axis=1, keepdims=True)
                halves.append((weights * (1.0 / whole)).astype(jnp.bfloat16))
            context = jnp.dot(
                jnp.concatenate(halves, axis=1), values, preferred_element_type=jnp.float32
            )
            out_ref[:, start + pair : start + pair + LANES] = context.astype(jnp.bfloat16)


def visit_context(visit, lengths, shards, gain, query, keyvals, cosine, sine):
    parts = len(shards)
    rows, features = shards[0].shape
    columns = query.shape[2]
    vmem = pl.BlockSpec(memory_space=pltpu.VMEM)
    operands = (*shards, gain, query, *keyvals, cosine, sine)
    return pl.pallas_call(
        functools.partial(visit_kernel, parts, visit),
        out_shape=jax.ShapeDtypeStruct((rows, columns), jnp.bfloat16),
        in_specs=[pl.BlockSpec(memory_space=pltpu.SMEM)] + [vmem] * len(operands),
        out_specs=vmem,
        scratch_shapes=[
            pltpu.VMEM((parts, rows, features), jnp.bfloat16),
            pltpu.VMEM((rows, columns), jnp.float32),
        ],
        compiler_params=pltpu.CompilerParams(vmem_limit_bytes=24 * 1024 * 1024),
        cost_estimate=pl.CostEstimate(
            flops=2 * rows * parts * features * (columns + LANES),
            bytes_accessed=2 * parts * features * columns,
            transcendentals=rows * rows * columns // HD,
        ),
        name=f"visit_{visit}",
    )(lengths, *operands)


def mean_kernel(lengths_ref, *refs):
    terms, out_ref = refs[:-1], refs[-1]
    rows = out_ref.shape[0]
    length = lengths_ref[lax.axis_index("snap")]
    total = terms[0][...].astype(jnp.float32)
    for term in terms[1:]:
        total += term[...].astype(jnp.float32)
    keep = lax.broadcasted_iota(jnp.int32, (rows, 1), 0) < length
    out_ref[...] = jnp.where(keep, total / len(terms), 0.0).astype(jnp.bfloat16)


def mean_of(lengths, terms):
    vmem = pl.BlockSpec(memory_space=pltpu.VMEM)
    return pl.pallas_call(
        mean_kernel,
        out_shape=jax.ShapeDtypeStruct(terms[0].shape, jnp.bfloat16),
        in_specs=[pl.BlockSpec(memory_space=pltpu.SMEM)] + [vmem] * len(terms),
        out_specs=vmem,
        name="mean_of_visits",
    )(lengths, *terms)


def on_device(block_states, lengths, norm_gain, query_weight, keyval_weight):
    snaps = lax.axis_size("snap")
    parts = lax.axis_size("tp")
    rank = lax.axis_index("tp")
    own = block_states[0]
    rows, features = own.shape
    gain = norm_gain[0].reshape(parts, features)
    query = query_weight[0].reshape(parts, features, query_weight.shape[2])
    heads_here = query.shape[2] // HD
    group = QHEADS // KVHEADS
    cosine, sine = rope_tables(rows)

    keyvals = []
    for bits in range(parts):
        head = (lax.bitwise_xor(rank, jnp.int32(bits)) * heads_here) // group
        columns = lax.dynamic_slice_in_dim(keyval_weight[0], head * 2 * HD, 2 * HD, 1)
        keyvals.append(swapped(columns, bits) if bits else columns)

    blocks = [own]
    for _ in range(1, VISITS):
        blocks.append(lax.ppermute(blocks[-1], "snap", ring_pairs(snaps, 1)))

    terms = [None] * VISITS
    for visit in (*range(1, VISITS), 0):
        shards = {0: blocks[visit]}
        for bits in range(2, parts, 2):
            shards[bits] = swapped(blocks[visit], bits)
        for bits in range(1, parts, 2):
            shards[bits] = swapped(shards[bits - 1], 1)
        context = visit_context(
            visit,
            lengths,
            [shards[bits] for bits in range(parts)],
            gain,
            query,
            keyvals,
            cosine,
            sine,
        )
        terms[visit] = (
            lax.ppermute(context, "snap", ring_pairs(snaps, -visit)) if visit else context
        )
    return mean_of(lengths, terms)[None]


def solution(mesh):
    placed = (
        P(("league", "snap"), None, "tp"),
        P("league"),
        P("snap", None),
        P("snap", None, "tp"),
        P("snap", "tp", None),
    )
    return jax.shard_map(
        on_device,
        mesh=mesh,
        in_specs=placed,
        out_specs=P(("league", "snap"), None, "tp"),
        check_vma=False,
    )
```

```python
import functools

import jax
import jax.numpy as jnp
import numpy as np
from jax import lax
from jax.experimental import pallas as pl
from jax.experimental.pallas import tpu as pltpu
from jax.sharding import PartitionSpec as P

QHEADS = 64
KVHEADS = 4
HD = 64
VISITS = 4
LANES = 128
VMEM_LIMIT = 16 * 1024 * 1024

EPSILON = 1e-05
ROPE_BASE = 500000.0
LOG2E = 1.4426950408889634


def visit_pairs(snaps, visit, back=False):
    if snaps == VISITS:
        return [(i, i ^ visit) for i in range(snaps)]
    return [(i, (i + (-visit if back else visit)) % snaps) for i in range(snaps)]


def visiting_block(snap, snaps, visit):
    if snaps == VISITS:
        return lax.bitwise_xor(snap, jnp.int32(visit))
    return lax.rem(snap + (snaps - visit), snaps)


def swapped(array, with_bits):
    count = lax.axis_size("tp")
    return lax.ppermute(array, "tp", [(i, i ^ with_bits) for i in range(count)])


def rope_tables(row_count):
    half = HD // 2
    positions = np.arange(row_count, dtype=np.float32)[:, None]
    frequency = np.float32(ROPE_BASE) ** (-np.arange(half, dtype=np.float32) * np.float32(2.0 / HD))
    angles = positions * frequency[None, :].astype(np.float32)
    cosine, sine = np.cos(angles), np.sin(angles)
    repeats = LANES // HD
    return (
        jnp.asarray(np.concatenate([cosine, cosine] * repeats, axis=1)),
        jnp.asarray(np.concatenate([-sine, sine] * repeats, axis=1)),
    )


def rotated(pair, cosine, signed_sine, in_first_half):
    half = HD // 2
    partner = jnp.where(
        in_first_half, pltpu.roll(pair, LANES - half, 1), pltpu.roll(pair, half, 1)
    )
    return pair * cosine + partner * signed_sine


def visit_kernel(parts, visits, *refs):
    held = 1 + parts // 2
    blocks = [refs[number * held : (number + 1) * held] for number in range(visits)]
    refs = refs[visits * held :]
    gain_ref, query_ref, keyval_ref, cosine_ref, sine_ref = refs[:5]
    biases = refs[5 : 5 + visits]
    outs = refs[5 + visits : -4]
    normed_ref, queries_ref, scores_ref, probabilities_ref = refs[-4:]
    rows, features = blocks[0][0].shape
    columns = query_ref.shape[2]
    width = parts * features
    step = 2 * LANES
    pairs = columns // LANES
    rank = lax.axis_index("tp")
    spans = [slice(number * rows, (number + 1) * rows) for number in range(visits)]

    for (own, beside, *chips), span in zip(blocks, spans):
        shards = [(own, 0, rank), (beside, 0, lax.bitwise_xor(rank, jnp.int32(1)))]
        for number, chip in enumerate(chips):
            first = lax.bitwise_xor(rank, jnp.int32(2 * (number + 1)))
            first = first - lax.rem(first, 2)
            shards += [(chip, 0, first), (chip, rows, first + 1)]
        squares = jnp.zeros((rows, 1), jnp.float32)
        for shard, start, _ in shards:
            values = shard[start : start + rows].astype(jnp.float32)
            squares += jnp.sum(values * values, axis=1, keepdims=True)
        scale = lax.rsqrt(squares / width + EPSILON)
        for shard, start, owner in shards:
            values = shard[start : start + rows].astype(jnp.float32)
            gain = gain_ref[:, pl.ds(pl.multiple_of(owner * features, LANES), features)]
            normed_ref[owner, span] = (values * scale * gain).astype(jnp.bfloat16)
    keyval = jnp.zeros((visits * rows, keyval_ref.shape[2]), jnp.float32)
    for part in range(parts):
        keyval += jnp.dot(normed_ref[part], keyval_ref[part], preferred_element_type=jnp.float32)

    cosine, sine = cosine_ref[...], sine_ref[...]
    lane = lax.broadcasted_iota(jnp.int32, (rows, LANES), 1)
    in_first_half = lax.rem(lane, HD) < HD // 2
    in_first_head = lane < HD
    all_keys, all_values = [], []
    for span in spans:
        mine = keyval[span].astype(jnp.bfloat16).astype(jnp.float32)
        keys = jnp.where(in_first_head, rotated(mine, cosine, sine, in_first_half), 0.0)
        all_keys.append(
            jnp.concatenate([keys, pltpu.roll(keys, HD, 1)], axis=0).astype(jnp.bfloat16)
        )
        values = jnp.where(in_first_head, 0.0, mine)
        values = jnp.concatenate([pltpu.roll(values, HD, 1), values], axis=0)
        all_values.append(values.T.astype(jnp.bfloat16))

    for start in range(0, columns, step):
        total = jnp.zeros((visits * rows, step), jnp.float32)
        for part in range(parts):
            total += jnp.dot(
                normed_ref[part],
                query_ref[part, :, start : start + step],
                preferred_element_type=jnp.float32,
            )
        for pair in range(0, step, LANES):
            for span in spans:
                queries_ref[span, start + pair : start + pair + LANES] = rotated(
                    total[span, pair : pair + LANES], cosine, sine, in_first_half
                ).astype(jnp.bfloat16)
    for number, span in enumerate(spans):
        for pair in range(pairs):
            scores_ref[number * pairs + pair] = lax.dot_general(
                all_keys[number],
                queries_ref[span, pair * LANES : (pair + 1) * LANES],
                (((1,), (1,)), ((), ())),
                preferred_element_type=jnp.float32,
            )
    for number in range(visits):
        for pair in range(number * pairs, (number + 1) * pairs):
            for head in range(2):
                mine = scores_ref[pair, head * rows : (head + 1) * rows] + biases[number][...]
                top = jnp.max(mine, axis=0, keepdims=True)
                weights = jnp.exp2((mine - top) * (LOG2E * HD**-0.5))
                whole = jnp.sum(weights, axis=0, keepdims=True)
                probabilities_ref[pair, head * rows : (head + 1) * rows] = (
                    weights * (1.0 / whole)
                ).astype(jnp.bfloat16)
    for number in range(visits):
        for pair in range(pairs):
            place = slice(pair * LANES, (pair + 1) * LANES)
            context = jnp.dot(
                all_values[number],
                probabilities_ref[number * pairs + pair],
                preferred_element_type=jnp.float32,
            )
            context = context.T.astype(jnp.bfloat16)
            outs[number][:, place] = context


def visit_contexts(blocks, biases, name, gain, query, keyval, cosine, sine):
    visits, parts = len(blocks), query.shape[0]
    rows, features = blocks[0][0].shape
    columns = query.shape[2]
    vmem = pl.BlockSpec(memory_space=pltpu.VMEM)
    operands = (
        *(shard for shards in blocks for shard in shards),
        gain,
        query,
        keyval,
        cosine,
        sine,
        *biases,
    )
    scores = (visits * columns // LANES, 2 * rows, rows)
    return pl.pallas_call(
        functools.partial(visit_kernel, parts, visits),
        out_shape=[pltpu.VMEM((rows, columns), jnp.bfloat16)] * visits,
        in_specs=[vmem] * len(operands),
        out_specs=[vmem] * visits,
        scratch_shapes=[
            pltpu.VMEM((parts, visits * rows, features), jnp.bfloat16),
            pltpu.VMEM((visits * rows, columns), jnp.bfloat16),
            pltpu.VMEM(scores, jnp.float32),
            pltpu.VMEM(scores, jnp.bfloat16),
        ],
        compiler_params=pltpu.CompilerParams(vmem_limit_bytes=VMEM_LIMIT),
        cost_estimate=pl.CostEstimate(flops=1, bytes_accessed=1, transcendentals=0),
        name=name,
    )(*operands)


def mean_kernel(keep_ref, *refs):
    terms, (out_any, out_ref, sems) = refs[:-3], refs[-3:]
    rows, _ = out_ref.shape
    strips = 2
    strip = rows // strips
    leaving = []
    for number in range(strips):
        place = pl.ds(number * strip, strip)
        total = terms[0][place].astype(jnp.float32)
        for term in terms[1:]:
            total += term[place].astype(jnp.float32)
        keep = keep_ref[place, :1] > 0.0
        out_ref[place] = jnp.where(keep, total / VISITS, 0.0).astype(jnp.bfloat16)
        leaving.append(
            pltpu.make_async_copy(out_ref.at[place], out_any.at[place], sems.at[number])
        )
        leaving[-1].start()
    for copy in leaving:
        copy.wait()


def mean_of(keep, terms):
    vmem = pl.BlockSpec(memory_space=pltpu.VMEM)
    operands = [pltpu.with_memory_space_constraint(term, pltpu.VMEM) for term in terms]
    return pl.pallas_call(
        mean_kernel,
        out_shape=jax.ShapeDtypeStruct(terms[0].shape, jnp.bfloat16),
        in_specs=[vmem] * (1 + len(operands)),
        out_specs=pl.BlockSpec(memory_space=pl.ANY),
        scratch_shapes=[
            pltpu.VMEM(terms[0].shape, jnp.bfloat16),
            pltpu.SemaphoreType.DMA((2,)),
        ],
        compiler_params=pltpu.CompilerParams(vmem_limit_bytes=VMEM_LIMIT),
        name="mean_of_visits",
    )(keep, *operands)


def stage_kernel(lengths_ref, query_any, gain_any, cosine_any, sine_any, *refs):
    query_ref, gain_ref, cosine_ref, sine_ref, keep_ref, token_ref, *biases = refs[:-1]
    sems = refs[-1]
    parts = query_ref.shape[0]
    moves = [(gain_any, gain_ref), (cosine_any, cosine_ref), (sine_any, sine_ref)]
    moves += [(query_any.at[part], query_ref.at[part]) for part in range(parts)]
    copies = [
        pltpu.make_async_copy(source, target, sems.at[number])
        for number, (source, target) in enumerate(moves)
    ]
    for copy in copies:
        copy.start()
    snap = lax.axis_index("snap")
    snaps = lax.axis_size("snap")
    rows = keep_ref.shape[0]
    token_ref[...] = jnp.zeros(token_ref.shape, token_ref.dtype)
    row = lax.broadcasted_iota(jnp.int32, keep_ref.shape, 0)
    keep_ref[...] = jnp.where(row < lengths_ref[snap], 1.0, 0.0)
    row = lax.broadcasted_iota(jnp.int32, (rows, rows), 1)
    key = lax.broadcasted_iota(jnp.int32, (rows, rows), 0)
    for visit, bias_ref in enumerate(biases):
        length = lengths_ref[visiting_block(snap, snaps, visit)]
        bias_ref[...] = jnp.where((key <= row) & (key < length), 0.0, -1e30)
    for copy in copies:
        copy.wait()


def staged(lengths, query, gain, cosine, sine, rows):
    hbm = pl.BlockSpec(memory_space=pltpu.HBM)
    vmem = pl.BlockSpec(memory_space=pltpu.VMEM)
    held = [(array.shape, array.dtype) for array in (query, gain, cosine, sine)]
    held += [((rows, LANES), jnp.float32)]
    biases = [((rows, rows), jnp.float32)] * VISITS
    return pl.pallas_call(
        stage_kernel,
        out_shape=[
            *(pltpu.VMEM(*each) for each in held),
            jax.ShapeDtypeStruct((8, LANES), jnp.float32),
            *(pltpu.VMEM(*each) for each in biases),
        ],
        in_specs=[pl.BlockSpec(memory_space=pltpu.SMEM)] + [hbm] * 4,
        out_specs=[vmem] * (len(held) + 1 + len(biases)),
        scratch_shapes=[pltpu.SemaphoreType.DMA((3 + query.shape[0],))],
        compiler_params=pltpu.CompilerParams(vmem_limit_bytes=VMEM_LIMIT),
        name="stage_weights",
    )(
        lengths,
        *(
            pltpu.with_memory_space_constraint(array, pltpu.HBM)
            for array in (query, gain, cosine, sine)
        ),
    )


def head_of(rank, heads_here):
    return (rank * heads_here) // (QHEADS // KVHEADS)


def cut_kernel(heads_here, keyval_ref, own_ref, beside_ref, *chip_refs):
    rank = lax.axis_index("tp")
    league = lax.axis_index("league")
    width = own_ref.shape[1]

    def columns(other):
        head = head_of(lax.bitwise_xor(rank, jnp.int32(other)), heads_here)
        return pl.ds(pl.multiple_of(head * width, LANES), width)

    own_ref[...] = keyval_ref[:, columns(0)]
    beside_ref[...] = keyval_ref[:, columns(1)]
    core = lax.rem(rank, 2)
    for number, chip_ref in enumerate(chip_refs):
        rows = chip_ref.shape[1]
        mine = pl.ds(pl.multiple_of(league * rows, 16), rows)
        for beside in range(2):
            chip_ref[lax.bitwise_xor(core, jnp.int32(beside))] = keyval_ref[
                mine, columns(2 * (number + 1) + beside)
            ]


def cut_keyval(keyval, heads_here, parts, leagues):
    features, width = keyval.shape[0], 2 * HD
    column = jax.ShapeDtypeStruct((features, width), keyval.dtype)
    chip = jax.ShapeDtypeStruct((2, features // leagues, width), keyval.dtype)
    chips = parts // 2 - 1
    vmem = pl.BlockSpec(memory_space=pltpu.VMEM)
    return pl.pallas_call(
        functools.partial(cut_kernel, heads_here),
        out_shape=[column, column] + [chip] * chips,
        in_specs=[vmem],
        out_specs=[vmem] * (2 + chips),
        compiler_params=pltpu.CompilerParams(vmem_limit_bytes=VMEM_LIMIT),
        name="cut_keyval",
    )(keyval)


def join_kernel(leagues, own_ref, beside_ref, *refs):
    pieces, out_ref, sems = refs[:-2], refs[-2], refs[-1]
    rank = lax.axis_index("tp")
    league = lax.axis_index("league")
    core = lax.rem(rank, 2)
    copies = [(own_ref, out_ref.at[rank]), (beside_ref, out_ref.at[lax.bitwise_xor(rank, 1)])]
    number = 0
    for chip in range(1, out_ref.shape[0] // 2):
        for beside in range(2):
            owner = lax.bitwise_xor(rank, jnp.int32(2 * chip + beside))
            for by in range(leagues):
                piece = pieces[number]
                rows = piece.shape[1]
                source = lax.rem(league + (leagues - by), leagues)
                place = pl.ds(pl.multiple_of(source * rows, 16), rows)
                copies.append((piece.at[core], out_ref.at[owner, place]))
                number += 1
    started = [
        pltpu.make_async_copy(source, target, sems.at[i])
        for i, (source, target) in enumerate(copies)
    ]
    for copy in started:
        copy.start()
    for copy in started:
        copy.wait()


def join_keyval(own, beside, pieces, parts, leagues):
    any_space = pl.BlockSpec(memory_space=pl.ANY)
    return pl.pallas_call(
        functools.partial(join_kernel, leagues),
        out_shape=pltpu.VMEM((parts, *own.shape), own.dtype),
        in_specs=[any_space] * (2 + len(pieces)),
        out_specs=pl.BlockSpec(memory_space=pltpu.VMEM),
        scratch_shapes=[pltpu.SemaphoreType.DMA((2 + len(pieces),))],
        compiler_params=pltpu.CompilerParams(vmem_limit_bytes=VMEM_LIMIT),
        name="join_keyval",
    )(own, beside, *pieces)


def kept_order(array, *earlier):
    return lax.optimization_barrier((array, *earlier))[0]


def on_device(block_states, lengths, norm_gain, query_weight, keyval_weight):
    snaps = lax.axis_size("snap")
    parts = lax.axis_size("tp")
    leagues = lax.axis_size("league")
    own = block_states[0]
    rows, features = own.shape
    query = query_weight[0].reshape(parts, features, query_weight.shape[2])
    heads_here = query.shape[2] // HD
    cosine, sine = rope_tables(rows)

    own_columns, beside_columns, *chip_columns = cut_keyval(
        keyval_weight[0], heads_here, parts, leagues
    )
    query_held, gain_held, cosine_held, sine_held, keep, token, *biases = staged(
        lengths, query, norm_gain, cosine, sine, rows
    )
    def moved(block, visit):
        return lax.ppermute(block, "snap", visit_pairs(snaps, visit))

    if snaps == VISITS:
        block_2 = moved(own, 2)
        block_1 = moved(own, 1)
        block_3 = moved(block_2, 1)
    else:
        block_1 = moved(own, 1)
        block_2 = moved(block_1, 1)
        block_3 = moved(block_2, 1)
    beside = swapped(beside_columns, 1)
    arrived = [swapped(columns, 2 * (i + 1)) for i, columns in enumerate(chip_columns)]
    pieces = []
    for columns in arrived:
        by_league = [kept_order(columns, token)]
        for _ in range(1, leagues):
            by_league.append(lax.ppermute(by_league[-1], "league", [(i, (i + 1) % leagues) for i in range(leagues)]))
        pieces += by_league + [swapped(piece, 1) for piece in by_league]
    keyval = join_keyval(own_columns, beside, pieces, parts, leagues)

    def over_chips(block):
        return [block] + [swapped(block, bits) for bits in range(2, parts, 2)]

    pairs_of_cores = [[i, i + 1] for i in range(0, parts, 2)]

    def over_cores(shards, *earlier):
        own_shard, *chips = shards
        gathered = [own_shard, swapped(own_shard, 1)]
        for shard in chips:
            shard = kept_order(shard, *earlier) if earlier else shard
            gathered.append(
                lax.all_gather(shard, "tp", axis=0, tiled=True, axis_index_groups=pairs_of_cores)
            )
        return gathered

    def scored(visits, blocks):
        return visit_contexts(
            blocks,
            [biases[visit] for visit in visits],
            "visit_" + "_".join(str(visit) for visit in visits),
            gain_held,
            query_held,
            keyval,
            cosine_held,
            sine_held,
        )

    def sent_home(visit, array):
        return lax.ppermute(array, "snap", visit_pairs(snaps, visit, back=True))

    shards_2 = over_chips(kept_order(block_2, token, *arrived))
    shards_3 = over_chips(kept_order(block_3, *shards_2[1:]))
    [context_2] = scored([2], [over_cores(shards_2)])
    shards_1 = over_chips(kept_order(block_1, context_2, *shards_3[1:]))
    shards_0 = over_chips(kept_order(own, *shards_1[1:]))
    home_2 = sent_home(2, context_2)
    [context_3] = scored([3], [over_cores(shards_3, context_2)])
    home_3 = sent_home(3, context_3)
    [context_1] = scored([1], [over_cores(shards_1, context_3)])
    home_1 = sent_home(1, context_1)
    [context_0] = scored([0], [over_cores(shards_0, context_1)])
    return mean_of(keep, [context_0, home_1, home_2, home_3])[None]


def solution(mesh):
    placed = (
        P(("league", "snap"), None, "tp"),
        P("league"),
        P("snap", None),
        P("snap", None, "tp"),
        P("snap", "tp", None),
    )
    return jax.shard_map(
        on_device,
        mesh=mesh,
        in_specs=placed,
        out_specs=P(("league", "snap"), None, "tp"),
        check_vma=False,
    )

NEWGAIN=1
```

```python
import functools

import jax
import jax.numpy as jnp
import numpy as np
from jax import lax
from jax.experimental import pallas as pl
from jax.experimental.pallas import tpu as pltpu
from jax.sharding import PartitionSpec as P

QHEADS = 64
KVHEADS = 4
HD = 64
VISITS = 4
LANES = 128
VMEM_LIMIT = 16 * 1024 * 1024

EPSILON = 1e-05
ROPE_BASE = 500000.0
LOG2E = 1.4426950408889634


def visit_pairs(snaps, visit, back=False):
    if snaps == VISITS:
        return [(i, i ^ visit) for i in range(snaps)]
    return [(i, (i + (-visit if back else visit)) % snaps) for i in range(snaps)]


def visiting_block(snap, snaps, visit):
    if snaps == VISITS:
        return lax.bitwise_xor(snap, jnp.int32(visit))
    return lax.rem(snap + (snaps - visit), snaps)


def swapped(array, with_bits):
    count = lax.axis_size("tp")
    return lax.ppermute(array, "tp", [(i, i ^ with_bits) for i in range(count)])


def rope_tables(row_count):
    half = HD // 2
    positions = np.arange(row_count, dtype=np.float32)[:, None]
    frequency = np.float32(ROPE_BASE) ** (-np.arange(half, dtype=np.float32) * np.float32(2.0 / HD))
    angles = positions * frequency[None, :].astype(np.float32)
    cosine, sine = np.cos(angles), np.sin(angles)
    repeats = LANES // HD
    return (
        jnp.asarray(np.concatenate([cosine, cosine] * repeats, axis=1)),
        jnp.asarray(np.concatenate([-sine, sine] * repeats, axis=1)),
    )


def rotated(pair, cosine, signed_sine, in_first_half):
    half = HD // 2
    partner = jnp.where(
        in_first_half, pltpu.roll(pair, LANES - half, 1), pltpu.roll(pair, half, 1)
    )
    return pair * cosine + partner * signed_sine


def visit_kernel(parts, held, *refs):
    (own, beside, *chips), refs = refs[:held], refs[held:]
    gain_ref, query_ref, keyval_ref, cosine_ref, sine_ref, bias_ref = refs[:6]
    out_ref, normed_ref, queries_ref, scores_ref, probabilities_ref = refs[6:]
    rows, features = own.shape
    columns = query_ref.shape[2]
    width = parts * features
    step = 2 * LANES
    pairs = columns // LANES
    rank = lax.axis_index("tp")

    shards = [(own, 0, rank), (beside, 0, lax.bitwise_xor(rank, jnp.int32(1)))]
    if held == parts:
        for bits, shard in enumerate(chips, 2):
            shards.append((shard, 0, lax.bitwise_xor(rank, jnp.int32(bits))))
    else:
        for number, chip in enumerate(chips):
            first = lax.bitwise_xor(rank, jnp.int32(2 * (number + 1)))
            first = first - lax.rem(first, 2)
            shards += [(chip, 0, first), (chip, rows, first + 1)]

    squares = jnp.zeros((rows, 1), jnp.float32)
    for shard, start, _ in shards:
        values = shard[start : start + rows].astype(jnp.float32)
        squares += jnp.sum(values * values, axis=1, keepdims=True)
    scale = lax.rsqrt(squares / width + EPSILON)
    for shard, start, owner in shards:
        values = shard[start : start + rows].astype(jnp.float32)
        gain = gain_ref[:, pl.ds(pl.multiple_of(owner * features, LANES), features)]
        normed_ref[owner] = (values * scale * gain).astype(jnp.bfloat16)
    keyval = jnp.zeros((rows, keyval_ref.shape[2]), jnp.float32)
    for part in range(parts):
        keyval += jnp.dot(normed_ref[part], keyval_ref[part], preferred_element_type=jnp.float32)

    cosine, sine = cosine_ref[...], sine_ref[...]
    lane = lax.broadcasted_iota(jnp.int32, (rows, LANES), 1)
    in_first_half = lax.rem(lane, HD) < HD // 2
    in_first_head = lane < HD
    keyval = keyval.astype(jnp.bfloat16).astype(jnp.float32)
    keys = jnp.where(in_first_head, rotated(keyval, cosine, sine, in_first_half), 0.0)
    keys = jnp.concatenate([keys, pltpu.roll(keys, HD, 1)], axis=0).astype(jnp.bfloat16)
    values = jnp.where(in_first_head, 0.0, keyval)
    values = jnp.concatenate([pltpu.roll(values, HD, 1), values], axis=0).T.astype(jnp.bfloat16)

    for start in range(0, columns, step):
        total = jnp.zeros((rows, step), jnp.float32)
        for part in range(parts):
            total += jnp.dot(
                normed_ref[part],
                query_ref[part, :, start : start + step],
                preferred_element_type=jnp.float32,
            )
        for pair in range(0, step, LANES):
            queries_ref[:, start + pair : start + pair + LANES] = rotated(
                total[:, pair : pair + LANES], cosine, sine, in_first_half
            ).astype(jnp.bfloat16)
    for pair in range(pairs):
        scores_ref[pair] = lax.dot_general(
            keys,
            queries_ref[:, pair * LANES : (pair + 1) * LANES],
            (((1,), (1,)), ((), ())),
            preferred_element_type=jnp.float32,
        )
    for pair in range(pairs):
        for head in range(2):
            place = slice(head * rows, (head + 1) * rows)
            mine = scores_ref[pair, place] + bias_ref[...]
            top = jnp.max(mine, axis=0, keepdims=True)
            weights = jnp.exp2((mine - top) * (LOG2E * HD**-0.5))
            whole = jnp.sum(weights, axis=0, keepdims=True)
            probabilities_ref[pair, place] = (weights * (1.0 / whole)).astype(jnp.bfloat16)
    for pair in range(pairs):
        context = jnp.dot(values, probabilities_ref[pair], preferred_element_type=jnp.float32)
        out_ref[:, pair * LANES : (pair + 1) * LANES] = context.T.astype(jnp.bfloat16)


def visit_context(visit, shards, gain, query, keyval, cosine, sine, bias):
    parts, features, columns = query.shape
    rows = shards[0].shape[0]
    vmem = pl.BlockSpec(memory_space=pltpu.VMEM)
    operands = (*shards, gain, query, keyval, cosine, sine, bias)
    scores = (columns // LANES, 2 * rows, rows)
    return pl.pallas_call(
        functools.partial(visit_kernel, parts, len(shards)),
        out_shape=pltpu.VMEM((rows, columns), jnp.bfloat16),
        in_specs=[vmem] * len(operands),
        out_specs=vmem,
        scratch_shapes=[
            pltpu.VMEM((parts, rows, features), jnp.bfloat16),
            pltpu.VMEM((rows, columns), jnp.bfloat16),
            pltpu.VMEM(scores, jnp.float32),
            pltpu.VMEM(scores, jnp.bfloat16),
        ],
        compiler_params=pltpu.CompilerParams(vmem_limit_bytes=VMEM_LIMIT),
        cost_estimate=pl.CostEstimate(flops=1, bytes_accessed=1, transcendentals=0),
        name=f"visit_{visit}",
    )(*operands)


def mean_kernel(keep_ref, *refs):
    terms, (out_any, out_ref, sems) = refs[:-3], refs[-3:]
    rows, _ = out_ref.shape
    strips = 2
    strip = rows // strips
    leaving = []
    for number in range(strips):
        place = pl.ds(number * strip, strip)
        total = terms[0][place].astype(jnp.float32)
        for term in terms[1:]:
            total += term[place].astype(jnp.float32)
        keep = keep_ref[place, :1] > 0.0
        out_ref[place] = jnp.where(keep, total / VISITS, 0.0).astype(jnp.bfloat16)
        leaving.append(
            pltpu.make_async_copy(out_ref.at[place], out_any.at[place], sems.at[number])
        )
        leaving[-1].start()
    for copy in leaving:
        copy.wait()


def mean_of(keep, terms):
    vmem = pl.BlockSpec(memory_space=pltpu.VMEM)
    operands = [pltpu.with_memory_space_constraint(term, pltpu.VMEM) for term in terms]
    return pl.pallas_call(
        mean_kernel,
        out_shape=jax.ShapeDtypeStruct(terms[0].shape, jnp.bfloat16),
        in_specs=[vmem] * (1 + len(operands)),
        out_specs=pl.BlockSpec(memory_space=pl.ANY),
        scratch_shapes=[
            pltpu.VMEM(terms[0].shape, jnp.bfloat16),
            pltpu.SemaphoreType.DMA((2,)),
        ],
        compiler_params=pltpu.CompilerParams(vmem_limit_bytes=VMEM_LIMIT),
        name="mean_of_visits",
    )(keep, *operands)


def stage_kernel(lengths_ref, query_any, gain_any, cosine_any, sine_any, *refs):
    query_ref, gain_ref, cosine_ref, sine_ref, keep_ref, token_ref, *biases = refs[:-1]
    sems = refs[-1]
    parts = query_ref.shape[0]
    moves = [(gain_any, gain_ref), (cosine_any, cosine_ref), (sine_any, sine_ref)]
    moves += [(query_any.at[part], query_ref.at[part]) for part in range(parts)]
    copies = [
        pltpu.make_async_copy(source, target, sems.at[number])
        for number, (source, target) in enumerate(moves)
    ]
    for copy in copies:
        copy.start()
    snap = lax.axis_index("snap")
    snaps = lax.axis_size("snap")
    rows = keep_ref.shape[0]
    token_ref[...] = jnp.zeros(token_ref.shape, token_ref.dtype)
    row = lax.broadcasted_iota(jnp.int32, keep_ref.shape, 0)
    keep_ref[...] = jnp.where(row < lengths_ref[snap], 1.0, 0.0)
    row = lax.broadcasted_iota(jnp.int32, (rows, rows), 1)
    key = lax.broadcasted_iota(jnp.int32, (rows, rows), 0)
    for visit, bias_ref in enumerate(biases):
        length = lengths_ref[visiting_block(snap, snaps, visit)]
        bias_ref[...] = jnp.where((key <= row) & (key < length), 0.0, -1e30)
    for copy in copies:
        copy.wait()


def staged(lengths, query, gain, cosine, sine, rows):
    hbm = pl.BlockSpec(memory_space=pltpu.HBM)
    vmem = pl.BlockSpec(memory_space=pltpu.VMEM)
    held = [(array.shape, array.dtype) for array in (query, gain, cosine, sine)]
    held += [((rows, LANES), jnp.float32)]
    biases = [((rows, rows), jnp.float32)] * VISITS
    return pl.pallas_call(
        stage_kernel,
        out_shape=[
            *(pltpu.VMEM(*each) for each in held),
            jax.ShapeDtypeStruct((8, LANES), jnp.float32),
            *(pltpu.VMEM(*each) for each in biases),
        ],
        in_specs=[pl.BlockSpec(memory_space=pltpu.SMEM)] + [hbm] * 4,
        out_specs=[vmem] * (len(held) + 1 + len(biases)),
        scratch_shapes=[pltpu.SemaphoreType.DMA((3 + query.shape[0],))],
        compiler_params=pltpu.CompilerParams(vmem_limit_bytes=VMEM_LIMIT),
        name="stage_weights",
    )(
        lengths,
        *(
            pltpu.with_memory_space_constraint(array, pltpu.HBM)
            for array in (query, gain, cosine, sine)
        ),
    )


def head_of(rank, heads_here):
    return (rank * heads_here) // (QHEADS // KVHEADS)


def cut_kernel(heads_here, keyval_ref, own_ref, beside_ref, *chip_refs):
    rank = lax.axis_index("tp")
    league = lax.axis_index("league")
    width = own_ref.shape[1]

    def columns(other):
        head = head_of(lax.bitwise_xor(rank, jnp.int32(other)), heads_here)
        return pl.ds(pl.multiple_of(head * width, LANES), width)

    own_ref[...] = keyval_ref[:, columns(0)]
    beside_ref[...] = keyval_ref[:, columns(1)]
    core = lax.rem(rank, 2)
    for number, chip_ref in enumerate(chip_refs):
        rows = chip_ref.shape[1]
        mine = pl.ds(pl.multiple_of(league * rows, 16), rows)
        for beside in range(2):
            chip_ref[lax.bitwise_xor(core, jnp.int32(beside))] = keyval_ref[
                mine, columns(2 * (number + 1) + beside)
            ]


def cut_keyval(keyval, heads_here, parts, leagues):
    features, width = keyval.shape[0], 2 * HD
    column = jax.ShapeDtypeStruct((features, width), keyval.dtype)
    chip = jax.ShapeDtypeStruct((2, features // leagues, width), keyval.dtype)
    chips = parts // 2 - 1
    vmem = pl.BlockSpec(memory_space=pltpu.VMEM)
    return pl.pallas_call(
        functools.partial(cut_kernel, heads_here),
        out_shape=[column, column] + [chip] * chips,
        in_specs=[vmem],
        out_specs=[vmem] * (2 + chips),
        compiler_params=pltpu.CompilerParams(vmem_limit_bytes=VMEM_LIMIT),
        name="cut_keyval",
    )(keyval)


def join_kernel(leagues, own_ref, beside_ref, *refs):
    pieces, out_ref, sems = refs[:-2], refs[-2], refs[-1]
    rank = lax.axis_index("tp")
    league = lax.axis_index("league")
    core = lax.rem(rank, 2)
    copies = [(own_ref, out_ref.at[rank]), (beside_ref, out_ref.at[lax.bitwise_xor(rank, 1)])]
    number = 0
    for chip in range(1, out_ref.shape[0] // 2):
        for beside in range(2):
            owner = lax.bitwise_xor(rank, jnp.int32(2 * chip + beside))
            for by in range(leagues):
                piece = pieces[number]
                rows = piece.shape[1]
                source = lax.rem(league + (leagues - by), leagues)
                place = pl.ds(pl.multiple_of(source * rows, 16), rows)
                copies.append((piece.at[core], out_ref.at[owner, place]))
                number += 1
    started = [
        pltpu.make_async_copy(source, target, sems.at[i])
        for i, (source, target) in enumerate(copies)
    ]
    for copy in started:
        copy.start()
    for copy in started:
        copy.wait()


def join_keyval(own, beside, pieces, parts, leagues):
    any_space = pl.BlockSpec(memory_space=pl.ANY)
    return pl.pallas_call(
        functools.partial(join_kernel, leagues),
        out_shape=pltpu.VMEM((parts, *own.shape), own.dtype),
        in_specs=[any_space] * (2 + len(pieces)),
        out_specs=pl.BlockSpec(memory_space=pltpu.VMEM),
        scratch_shapes=[pltpu.SemaphoreType.DMA((2 + len(pieces),))],
        compiler_params=pltpu.CompilerParams(vmem_limit_bytes=VMEM_LIMIT),
        name="join_keyval",
    )(own, beside, *pieces)


def kept_order(array, *earlier):
    return lax.optimization_barrier((array, *earlier))[0]


def on_device(block_states, lengths, norm_gain, query_weight, keyval_weight):
    snaps = lax.axis_size("snap")
    parts = lax.axis_size("tp")
    leagues = lax.axis_size("league")
    own = block_states[0]
    rows, features = own.shape
    query = query_weight[0].reshape(parts, features, query_weight.shape[2])
    heads_here = query.shape[2] // HD
    cosine, sine = rope_tables(rows)

    own_columns, beside_columns, *chip_columns = cut_keyval(
        keyval_weight[0], heads_here, parts, leagues
    )
    query_held, gain_held, cosine_held, sine_held, keep, token, *biases = staged(
        lengths, query, norm_gain, cosine, sine, rows
    )
    def moved(block, visit):
        return lax.ppermute(block, "snap", visit_pairs(snaps, visit))

    if snaps == VISITS:
        block_2 = moved(own, 2)
        block_1 = moved(own, 1)
        block_3 = moved(block_2, 1)
    else:
        block_1 = moved(own, 1)
        block_2 = moved(block_1, 1)
        block_3 = moved(block_2, 1)
    beside = swapped(beside_columns, 1)
    arrived = [swapped(columns, 2 * (i + 1)) for i, columns in enumerate(chip_columns)]
    pieces = []
    for columns in arrived:
        by_league = [kept_order(columns, token, block_2)]
        for _ in range(1, leagues):
            by_league.append(lax.ppermute(by_league[-1], "league", [(i, (i + 1) % leagues) for i in range(leagues)]))
        pieces += by_league + [swapped(piece, 1) for piece in by_league]
    keyval = join_keyval(own_columns, beside, pieces, parts, leagues)

    def over_chips(block):
        return [block] + [swapped(block, bits) for bits in range(2, parts, 2)]

    pairs_of_cores = [[i, i + 1] for i in range(0, parts, 2)]

    def over_cores(shards, *earlier, apart=False):
        own_shard, *chips = shards
        gathered = [own_shard, swapped(own_shard, 1)]
        for shard in chips:
            shard = kept_order(shard, *earlier) if earlier else shard
            if apart:
                gathered += [shard, swapped(shard, 1)]
            else:
                gathered.append(
                    lax.all_gather(shard, "tp", axis=0, tiled=True, axis_index_groups=pairs_of_cores)
                )
        return gathered

    def scored(visit, shards):
        return visit_context(
            visit, shards, gain_held, query_held, keyval, cosine_held, sine_held, biases[visit]
        )

    def sent_home(visit, array):
        return lax.ppermute(array, "snap", visit_pairs(snaps, visit, back=True))

    shards_2 = over_chips(kept_order(block_2, token, *arrived))
    shards_3 = over_chips(kept_order(block_3, *shards_2[1:]))
    context_2 = scored(2, over_cores(shards_2, block_1, apart=True))
    home_2 = sent_home(2, context_2)
    shards_1 = over_chips(kept_order(block_1, context_2))
    shards_0 = over_chips(kept_order(own, *shards_1[1:]))
    context_3 = scored(3, over_cores(shards_3, context_2))
    home_3 = sent_home(3, context_3)
    context_1 = scored(1, over_cores(shards_1, context_3))
    home_1 = sent_home(1, context_1)
    context_0 = scored(0, over_cores(shards_0, context_1))
    return mean_of(keep, [context_0, home_1, home_2, home_3])[None]


def solution(mesh):
    placed = (
        P(("league", "snap"), None, "tp"),
        P("league"),
        P("snap", None),
        P("snap", None, "tp"),
        P("snap", "tp", None),
    )
    return jax.shard_map(
        on_device,
        mesh=mesh,
        in_specs=placed,
        out_specs=P(("league", "snap"), None, "tp"),
        check_vma=False,
    )
```

```python
import functools

import jax
import jax.numpy as jnp
import numpy as np
from jax import lax
from jax.experimental import pallas as pl
from jax.experimental.pallas import tpu as pltpu
from jax.sharding import PartitionSpec as P

QHEADS = 64
KVHEADS = 4
HD = 64
VISITS = 4
LANES = 128
STRIPS = 4
VMEM_LIMIT = 16 * 1024 * 1024

EPSILON = 1e-05
ROPE_BASE = 500000.0
LOG2E = 1.4426950408889634


def visit_pairs(snaps, visit, back=False):
    if snaps == VISITS:
        return [(i, i ^ visit) for i in range(snaps)]
    return [(i, (i + (-visit if back else visit)) % snaps) for i in range(snaps)]


def visiting_block(snap, snaps, visit):
    if snaps == VISITS:
        return lax.bitwise_xor(snap, jnp.int32(visit))
    return lax.rem(snap + (snaps - visit), snaps)


def swapped(array, with_bits):
    count = lax.axis_size("tp")
    return lax.ppermute(array, "tp", [(i, i ^ with_bits) for i in range(count)])


def rope_tables(row_count):
    half = HD // 2
    positions = np.arange(row_count, dtype=np.float32)[:, None]
    frequency = np.float32(ROPE_BASE) ** (-np.arange(half, dtype=np.float32) * np.float32(2.0 / HD))
    angles = positions * frequency[None, :].astype(np.float32)
    cosine, sine = np.cos(angles), np.sin(angles)
    repeats = LANES // HD
    return (
        jnp.asarray(np.concatenate([cosine, cosine] * repeats, axis=1)),
        jnp.asarray(np.concatenate([-sine, sine] * repeats, axis=1)),
    )


def rotated(pair, cosine, signed_sine, in_first_half):
    half = HD // 2
    partner = jnp.where(
        in_first_half, pltpu.roll(pair, LANES - half, 1), pltpu.roll(pair, half, 1)
    )
    return pair * cosine + partner * signed_sine


def visit_kernel(parts, held, *refs):
    (own, beside, *chips), refs = refs[:held], refs[held:]
    gain_ref, query_ref, keyval_ref, cosine_ref, sine_ref, bias_ref = refs[:6]
    out_ref, total_ref, queries_ref, scores_ref, probabilities_ref = refs[6:]
    rows, features = own.shape
    columns = query_ref.shape[2]
    width = parts * features
    step = 2 * LANES
    pairs = columns // LANES
    rank = lax.axis_index("tp")

    shards = [(own, 0, rank), (beside, 0, lax.bitwise_xor(rank, jnp.int32(1)))]
    if held == parts:
        for bits, shard in enumerate(chips, 2):
            shards.append((shard, 0, lax.bitwise_xor(rank, jnp.int32(bits))))
    else:
        for number, chip in enumerate(chips):
            first = lax.bitwise_xor(rank, jnp.int32(2 * (number + 1)))
            first = first - lax.rem(first, 2)
            shards += [(chip, 0, first), (chip, rows, first + 1)]

    squares = jnp.zeros((rows, 1), jnp.float32)
    for shard, start, _ in shards:
        values = shard[start : start + rows].astype(jnp.float32)
        squares += jnp.sum(values * values, axis=1, keepdims=True)
    scale = lax.rsqrt(squares / width + EPSILON)
    keyval = jnp.zeros((rows, keyval_ref.shape[2]), jnp.float32)

    def multiply(normed, owner, first):
        for start in range(0, columns, step):
            place = slice(start, start + step)
            product = jnp.dot(
                normed, query_ref[owner, :, place], preferred_element_type=jnp.float32
            )
            if first:
                total_ref[:, place] = product
            else:
                total_ref[:, place] += product
        return jnp.dot(normed, keyval_ref[owner], preferred_element_type=jnp.float32)

    for number, (shard, start, owner) in enumerate(shards):
        values = shard[start : start + rows].astype(jnp.float32)
        gain = gain_ref[:, pl.ds(pl.multiple_of(owner * features, LANES), features)]
        normed = (values * scale * gain).astype(jnp.bfloat16)
        keyval += multiply(normed, owner, number == 0)

    cosine, sine = cosine_ref[...], sine_ref[...]
    lane = lax.broadcasted_iota(jnp.int32, (rows, LANES), 1)
    in_first_half = lax.rem(lane, HD) < HD // 2
    in_first_head = lane < HD
    keyval = keyval.astype(jnp.bfloat16).astype(jnp.float32)
    keys = jnp.where(in_first_head, rotated(keyval, cosine, sine, in_first_half), 0.0)
    keys = jnp.concatenate([keys, pltpu.roll(keys, HD, 1)], axis=0).astype(jnp.bfloat16)
    values = jnp.where(in_first_head, 0.0, keyval)
    values = jnp.concatenate([pltpu.roll(values, HD, 1), values], axis=0).T.astype(jnp.bfloat16)

    for pair in range(pairs):
        place = slice(pair * LANES, (pair + 1) * LANES)
        queries_ref[:, place] = rotated(total_ref[:, place], cosine, sine, in_first_half).astype(
            jnp.bfloat16
        )
    for pair in range(pairs):
        scores_ref[pair] = lax.dot_general(
            keys,
            queries_ref[:, pair * LANES : (pair + 1) * LANES],
            (((1,), (1,)), ((), ())),
            preferred_element_type=jnp.float32,
        )
    for pair in range(pairs):
        for head in range(2):
            place = slice(head * rows, (head + 1) * rows)
            mine = scores_ref[pair, place] + bias_ref[...]
            top = jnp.max(mine, axis=0, keepdims=True)
            weights = jnp.exp2((mine - top) * (LOG2E * HD**-0.5))
            whole = jnp.sum(weights, axis=0, keepdims=True)
            probabilities_ref[pair, place] = (weights * (1.0 / whole)).astype(jnp.bfloat16)
    for pair in range(pairs):
        context = jnp.dot(values, probabilities_ref[pair], preferred_element_type=jnp.float32)
        out_ref[:, pair * LANES : (pair + 1) * LANES] = context.T.astype(jnp.bfloat16)


def visit_context(visit, shards, gain, query, keyval, cosine, sine, bias):
    parts, features, columns = query.shape
    rows = shards[0].shape[0]
    vmem = pl.BlockSpec(memory_space=pltpu.VMEM)
    operands = (*shards, gain, query, keyval, cosine, sine, bias)
    scores = (columns // LANES, 2 * rows, rows)
    return pl.pallas_call(
        functools.partial(visit_kernel, parts, len(shards)),
        out_shape=pltpu.VMEM((rows, columns), jnp.bfloat16),
        in_specs=[vmem] * len(operands),
        out_specs=vmem,
        scratch_shapes=[
            pltpu.VMEM((rows, columns), jnp.float32),
            pltpu.VMEM((rows, columns), jnp.bfloat16),
            pltpu.VMEM(scores, jnp.float32),
            pltpu.VMEM(scores, jnp.bfloat16),
        ],
        compiler_params=pltpu.CompilerParams(vmem_limit_bytes=VMEM_LIMIT),
        cost_estimate=pl.CostEstimate(flops=1, bytes_accessed=1, transcendentals=0),
        name=f"visit_{visit}",
    )(*operands)


def mean_kernel(keep_ref, *refs):
    terms, (out_any, out_ref, sems) = refs[:-3], refs[-3:]
    rows, _ = out_ref.shape
    strips = 2
    strip = rows // strips
    leaving = []
    for number in range(strips):
        place = pl.ds(number * strip, strip)
        total = terms[0][place].astype(jnp.float32)
        for term in terms[1:]:
            total += term[place].astype(jnp.float32)
        keep = keep_ref[place, :1] > 0.0
        out_ref[place] = jnp.where(keep, total / VISITS, 0.0).astype(jnp.bfloat16)
        leaving.append(
            pltpu.make_async_copy(out_ref.at[place], out_any.at[place], sems.at[number])
        )
        leaving[-1].start()
    for copy in leaving:
        copy.wait()


def mean_of(keep, terms):
    vmem = pl.BlockSpec(memory_space=pltpu.VMEM)
    operands = [pltpu.with_memory_space_constraint(term, pltpu.VMEM) for term in terms]
    return pl.pallas_call(
        mean_kernel,
        out_shape=jax.ShapeDtypeStruct(terms[0].shape, jnp.bfloat16),
        in_specs=[vmem] * (1 + len(operands)),
        out_specs=pl.BlockSpec(memory_space=pl.ANY),
        scratch_shapes=[
            pltpu.VMEM(terms[0].shape, jnp.bfloat16),
            pltpu.SemaphoreType.DMA((2,)),
        ],
        compiler_params=pltpu.CompilerParams(vmem_limit_bytes=VMEM_LIMIT),
        name="mean_of_visits",
    )(keep, *operands)


def stage_kernel(lengths_ref, query_any, gain_any, cosine_any, sine_any, *refs):
    query_ref, gain_ref, cosine_ref, sine_ref, keep_ref, token_ref, *biases = refs[:-1]
    sems = refs[-1]
    parts = query_ref.shape[0]
    moves = [(gain_any, gain_ref), (cosine_any, cosine_ref), (sine_any, sine_ref)]
    strip = query_ref.shape[1] // STRIPS
    for part in range(parts):
        for number in range(STRIPS):
            place = pl.ds(number * strip, strip)
            moves.append((query_any.at[part, place], query_ref.at[part, place]))
    copies = [
        pltpu.make_async_copy(source, target, sems.at[number])
        for number, (source, target) in enumerate(moves)
    ]
    for copy in copies:
        copy.start()
    snap = lax.axis_index("snap")
    snaps = lax.axis_size("snap")
    rows = keep_ref.shape[0]
    token_ref[...] = jnp.zeros(token_ref.shape, token_ref.dtype)
    row = lax.broadcasted_iota(jnp.int32, keep_ref.shape, 0)
    keep_ref[...] = jnp.where(row < lengths_ref[snap], 1.0, 0.0)
    row = lax.broadcasted_iota(jnp.int32, (rows, rows), 1)
    key = lax.broadcasted_iota(jnp.int32, (rows, rows), 0)
    for visit, bias_ref in enumerate(biases):
        length = lengths_ref[visiting_block(snap, snaps, visit)]
        bias_ref[...] = jnp.where((key <= row) & (key < length), 0.0, -1e30)
    for copy in copies:
        copy.wait()


def staged(lengths, query, gain, cosine, sine, rows):
    hbm = pl.BlockSpec(memory_space=pltpu.HBM)
    vmem = pl.BlockSpec(memory_space=pltpu.VMEM)
    held = [(array.shape, array.dtype) for array in (query, gain, cosine, sine)]
    held += [((rows, LANES), jnp.float32)]
    biases = [((rows, rows), jnp.float32)] * VISITS
    return pl.pallas_call(
        stage_kernel,
        out_shape=[
            *(pltpu.VMEM(*each) for each in held),
            jax.ShapeDtypeStruct((8, LANES), jnp.float32),
            *(pltpu.VMEM(*each) for each in biases),
        ],
        in_specs=[pl.BlockSpec(memory_space=pltpu.SMEM)] + [hbm] * 4,
        out_specs=[vmem] * (len(held) + 1 + len(biases)),
        scratch_shapes=[pltpu.SemaphoreType.DMA((3 + STRIPS * query.shape[0],))],
        compiler_params=pltpu.CompilerParams(vmem_limit_bytes=VMEM_LIMIT),
        name="stage_weights",
    )(
        lengths,
        *(
            pltpu.with_memory_space_constraint(array, pltpu.HBM)
            for array in (query, gain, cosine, sine)
        ),
    )


def head_of(rank, heads_here):
    return (rank * heads_here) // (QHEADS // KVHEADS)


def cut_kernel(heads_here, keyval_ref, *out_refs):
    rank = lax.axis_index("tp")
    league = lax.axis_index("league")
    for bits, out_ref in enumerate(out_refs):
        rows, width = out_ref.shape
        head = head_of(lax.bitwise_xor(rank, jnp.int32(bits)), heads_here)
        columns = pl.ds(pl.multiple_of(head * width, LANES), width)
        if bits < 2:
            out_ref[...] = keyval_ref[:, columns]
        else:
            out_ref[...] = keyval_ref[pl.ds(pl.multiple_of(league * rows, 16), rows), columns]


def cut_keyval(keyval, heads_here, parts, leagues):
    features, width = keyval.shape[0], 2 * HD
    rows = [features // (1 if bits < 2 else leagues) for bits in range(parts)]
    vmem = pl.BlockSpec(memory_space=pltpu.VMEM)
    return pl.pallas_call(
        functools.partial(cut_kernel, heads_here),
        out_shape=[jax.ShapeDtypeStruct((count, width), keyval.dtype) for count in rows],
        in_specs=[vmem],
        out_specs=[vmem] * parts,
        compiler_params=pltpu.CompilerParams(vmem_limit_bytes=VMEM_LIMIT),
        name="cut_keyval",
    )(keyval)


def join_kernel(counts, *refs):
    passed = (len(refs) - 2 - sum(counts)) // 2
    pieces, refs = refs[: sum(counts)], refs[sum(counts) :]
    sources, out_ref, targets, sems = (
        refs[:passed],
        refs[passed],
        refs[passed + 1 : -1],
        refs[-1],
    )
    rank = lax.axis_index("tp")
    league = lax.axis_index("league")
    moves = []
    for bits, count in enumerate(counts):
        owner = lax.bitwise_xor(rank, jnp.int32(bits))
        for by in range(count):
            piece = pieces[len(moves)]
            rows = piece.shape[0]
            source = lax.rem(league + (count - by), count)
            place = pl.ds(pl.multiple_of(source * rows, 16), rows)
            moves.append((piece, out_ref.at[owner, place]))
    moves += list(zip(sources, targets))
    copies = [
        pltpu.make_async_copy(source, target, sems.at[number])
        for number, (source, target) in enumerate(moves)
    ]
    for copy in copies:
        copy.start()
    for copy in copies:
        copy.wait()


def join_keyval(groups, passed):
    any_space = pl.BlockSpec(memory_space=pl.ANY)
    pieces = [piece for group in groups for piece in group]
    features, width = pieces[0].shape
    keyval, *held = pl.pallas_call(
        functools.partial(join_kernel, [len(group) for group in groups]),
        out_shape=[
            pltpu.VMEM((len(groups), features, width), pieces[0].dtype),
            *(pltpu.VMEM(array.shape, array.dtype) for array in passed),
        ],
        in_specs=[any_space] * (len(pieces) + len(passed)),
        out_specs=[pl.BlockSpec(memory_space=pltpu.VMEM)] * (1 + len(passed)),
        scratch_shapes=[pltpu.SemaphoreType.DMA((len(pieces) + len(passed),))],
        compiler_params=pltpu.CompilerParams(vmem_limit_bytes=VMEM_LIMIT),
        name="join_keyval",
    )(*pieces, *passed)
    return keyval, held


def kept_order(array, *earlier):
    return lax.optimization_barrier((array, *earlier))[0]


def on_device(block_states, lengths, norm_gain, query_weight, keyval_weight):
    snaps = lax.axis_size("snap")
    parts = lax.axis_size("tp")
    leagues = lax.axis_size("league")
    own = block_states[0]
    rows, features = own.shape
    query = query_weight[0].reshape(parts, features, query_weight.shape[2])
    heads_here = query.shape[2] // HD
    cosine, sine = rope_tables(rows)

    def moved(block, visit):
        return lax.ppermute(block, "snap", visit_pairs(snaps, visit))

    def sent_home(visit, array):
        return lax.ppermute(array, "snap", visit_pairs(snaps, visit, back=True))

    if snaps == VISITS:
        block_2 = moved(own, 2)
        block_1 = moved(own, 1)
        block_3 = moved(block_2, 1)
    else:
        block_1 = moved(own, 1)
        block_2 = moved(block_1, 1)
        block_3 = moved(block_2, 1)

    query_held, gain_held, cosine_held, sine_held, keep, token, *biases = staged(
        lengths, query, norm_gain, cosine, sine, rows
    )

    columns = cut_keyval(keyval_weight[0], heads_here, parts, leagues)
    groups = [[columns[0]], [swapped(columns[1], 1)]]
    arrived = [swapped(columns[bits], bits) for bits in range(2, parts)]
    for piece in arrived:
        by_league = [kept_order(piece, token, block_1, block_2)]
        for _ in range(1, leagues):
            by_league.append(
                lax.ppermute(
                    by_league[-1], "league", [(i, (i + 1) % leagues) for i in range(leagues)]
                )
            )
        groups.append(by_league)

    def over_chips(block):
        return [block] + [swapped(block, bits) for bits in range(2, parts, 2)]

    pairs_of_cores = [[i, i + 1] for i in range(0, parts, 2)]

    def over_cores(shards, *earlier, apart=False):
        own_shard, *chips = shards
        gathered = [own_shard, swapped(own_shard, 1)]
        for shard in chips:
            shard = kept_order(shard, *earlier)
            if apart:
                gathered += [shard, swapped(shard, 1)]
            else:
                gathered.append(
                    lax.all_gather(shard, "tp", axis=0, tiled=True, axis_index_groups=pairs_of_cores)
                )
        return gathered

    shards_2 = over_chips(kept_order(block_2, token, *arrived))
    shards_3 = over_chips(kept_order(block_3, *shards_2[1:]))
    keyval, held = join_keyval(groups, shards_2[1:])

    def scored(visit, shards):
        return visit_context(
            visit, shards, gain_held, query_held, keyval, cosine_held, sine_held, biases[visit]
        )

    context_2 = scored(2, over_cores([shards_2[0], *held], block_1, apart=True))
    home_2 = sent_home(2, context_2)
    shards_1 = over_chips(kept_order(block_1, context_2))
    shards_0 = over_chips(kept_order(own, context_2, *shards_1[1:]))
    context_3 = scored(3, over_cores(shards_3, context_2))
    home_3 = sent_home(3, context_3)
    context_1 = scored(1, over_cores(shards_1, context_3))
    home_1 = sent_home(1, context_1)
    context_0 = scored(0, over_cores(shards_0, context_3))
    return mean_of(keep, [context_0, home_2, home_3, home_1])[None]


def solution(mesh):
    placed = (
        P(("league", "snap"), None, "tp"),
        P("league"),
        P("snap", None),
        P("snap", None, "tp"),
        P("snap", "tp", None),
    )
    return jax.shard_map(
        on_device,
        mesh=mesh,
        in_specs=placed,
        out_specs=P(("league", "snap"), None, "tp"),
        check_vma=False,
    )
```

```python
import functools

import jax
import jax.numpy as jnp
import numpy as np
from jax import lax
from jax.experimental import pallas as pl
from jax.experimental.pallas import tpu as pltpu
from jax.sharding import PartitionSpec as P

QHEADS = 64
KVHEADS = 4
HD = 64
VISITS = 4
LANES = 128
STRIPS = 4
VMEM_LIMIT = 16 * 1024 * 1024

EPSILON = 1e-05
ROPE_BASE = 500000.0
LOG2E = 1.4426950408889634


def visit_pairs(snaps, visit, back=False):
    if snaps == VISITS:
        return [(i, i ^ visit) for i in range(snaps)]
    return [(i, (i + (-visit if back else visit)) % snaps) for i in range(snaps)]


def visiting_block(snap, snaps, visit):
    if snaps == VISITS:
        return lax.bitwise_xor(snap, jnp.int32(visit))
    return lax.rem(snap + (snaps - visit), snaps)


def swapped(array, with_bits):
    count = lax.axis_size("tp")
    return lax.ppermute(array, "tp", [(i, i ^ with_bits) for i in range(count)])


def rope_tables(row_count):
    half = HD // 2
    positions = np.arange(row_count, dtype=np.float32)[:, None]
    frequency = np.float32(ROPE_BASE) ** (-np.arange(half, dtype=np.float32) * np.float32(2.0 / HD))
    angles = positions * frequency[None, :].astype(np.float32)
    cosine, sine = np.cos(angles), np.sin(angles)
    repeats = LANES // HD
    return (
        jnp.asarray(np.concatenate([cosine, cosine] * repeats, axis=1)),
        jnp.asarray(np.concatenate([-sine, sine] * repeats, axis=1)),
    )


def rotated(pair, cosine, signed_sine, in_first_half):
    half = HD // 2
    partner = jnp.where(
        in_first_half, pltpu.roll(pair, LANES - half, 1), pltpu.roll(pair, half, 1)
    )
    return pair * cosine + partner * signed_sine


def visit_kernel(parts, held, *refs):
    (own, beside, *chips), refs = refs[:held], refs[held:]
    gain_ref, query_ref, keyval_ref, cosine_ref, sine_ref, bias_ref = refs[:6]
    out_ref, total_ref, queries_ref, scores_ref, probabilities_ref = refs[6:]
    rows, features = own.shape
    columns = query_ref.shape[2]
    width = parts * features
    step = 2 * LANES
    pairs = columns // LANES
    rank = lax.axis_index("tp")

    shards = [(own, 0, rank), (beside, 0, lax.bitwise_xor(rank, jnp.int32(1)))]
    if held == parts:
        for bits, shard in enumerate(chips, 2):
            shards.append((shard, 0, lax.bitwise_xor(rank, jnp.int32(bits))))
    else:
        for number, chip in enumerate(chips):
            first = lax.bitwise_xor(rank, jnp.int32(2 * (number + 1)))
            first = first - lax.rem(first, 2)
            shards += [(chip, 0, first), (chip, rows, first + 1)]

    squares = jnp.zeros((rows, 1), jnp.float32)
    for shard, start, _ in shards:
        values = shard[start : start + rows].astype(jnp.float32)
        squares += jnp.sum(values * values, axis=1, keepdims=True)
    scale = lax.rsqrt(squares / width + EPSILON)
    keyval = jnp.zeros((rows, keyval_ref.shape[2]), jnp.float32)

    def multiply(normed, owner, first):
        for start in range(0, columns, step):
            place = slice(start, start + step)
            product = jnp.dot(
                normed, query_ref[owner, :, place], preferred_element_type=jnp.float32
            )
            if first:
                total_ref[:, place] = product
            else:
                total_ref[:, place] += product
        return jnp.dot(normed, keyval_ref[owner], preferred_element_type=jnp.float32)

    for number, (shard, start, owner) in enumerate(shards):
        values = shard[start : start + rows].astype(jnp.float32)
        gain = gain_ref[:, pl.ds(pl.multiple_of(owner * features, LANES), features)]
        normed = (values * scale * gain).astype(jnp.bfloat16)
        keyval += multiply(normed, owner, number == 0)

    cosine, sine = cosine_ref[...], sine_ref[...]
    lane = lax.broadcasted_iota(jnp.int32, (rows, LANES), 1)
    in_first_half = lax.rem(lane, HD) < HD // 2
    in_first_head = lane < HD
    keyval = keyval.astype(jnp.bfloat16).astype(jnp.float32)
    keys = jnp.where(in_first_head, rotated(keyval, cosine, sine, in_first_half), 0.0)
    keys = jnp.concatenate([keys, pltpu.roll(keys, HD, 1)], axis=0).astype(jnp.bfloat16)
    values = jnp.where(in_first_head, 0.0, keyval)
    values = jnp.concatenate([pltpu.roll(values, HD, 1), values], axis=0).T.astype(jnp.bfloat16)

    for pair in range(pairs):
        place = slice(pair * LANES, (pair + 1) * LANES)
        queries_ref[:, place] = rotated(total_ref[:, place], cosine, sine, in_first_half).astype(
            jnp.bfloat16
        )
    for pair in range(pairs):
        scores_ref[pair] = lax.dot_general(
            keys,
            queries_ref[:, pair * LANES : (pair + 1) * LANES],
            (((1,), (1,)), ((), ())),
            preferred_element_type=jnp.float32,
        )
    for pair in range(pairs):
        for head in range(2):
            place = slice(head * rows, (head + 1) * rows)
            mine = scores_ref[pair, place] + bias_ref[...]
            top = jnp.max(mine, axis=0, keepdims=True)
            weights = jnp.exp2((mine - top) * (LOG2E * HD**-0.5))
            whole = jnp.sum(weights, axis=0, keepdims=True)
            probabilities_ref[pair, place] = (weights * (1.0 / whole)).astype(jnp.bfloat16)
    for pair in range(pairs):
        context = jnp.dot(values, probabilities_ref[pair], preferred_element_type=jnp.float32)
        out_ref[:, pair * LANES : (pair + 1) * LANES] = context.T.astype(jnp.bfloat16)


def visit_context(visit, shards, gain, query, keyval, cosine, sine, bias):
    parts, features, columns = query.shape
    rows = shards[0].shape[0]
    vmem = pl.BlockSpec(memory_space=pltpu.VMEM)
    operands = (*shards, gain, query, keyval, cosine, sine, bias)
    scores = (columns // LANES, 2 * rows, rows)
    return pl.pallas_call(
        functools.partial(visit_kernel, parts, len(shards)),
        out_shape=pltpu.VMEM((rows, columns), jnp.bfloat16),
        in_specs=[vmem] * len(operands),
        out_specs=vmem,
        scratch_shapes=[
            pltpu.VMEM((rows, columns), jnp.float32),
            pltpu.VMEM((rows, columns), jnp.bfloat16),
            pltpu.VMEM(scores, jnp.float32),
            pltpu.VMEM(scores, jnp.bfloat16),
        ],
        compiler_params=pltpu.CompilerParams(vmem_limit_bytes=VMEM_LIMIT),
        cost_estimate=pl.CostEstimate(flops=1, bytes_accessed=1, transcendentals=0),
        name=f"visit_{visit}",
    )(*operands)


def mean_kernel(keep_ref, *refs):
    terms, (out_any, out_ref, sems) = refs[:-3], refs[-3:]
    rows, _ = out_ref.shape
    strips = 2
    strip = rows // strips
    leaving = []
    for number in range(strips):
        place = pl.ds(number * strip, strip)
        total = terms[0][place].astype(jnp.float32)
        for term in terms[1:]:
            total += term[place].astype(jnp.float32)
        keep = keep_ref[place, :1] > 0.0
        out_ref[place] = jnp.where(keep, total / VISITS, 0.0).astype(jnp.bfloat16)
        leaving.append(
            pltpu.make_async_copy(out_ref.at[place], out_any.at[place], sems.at[number])
        )
        leaving[-1].start()
    for copy in leaving:
        copy.wait()


def mean_of(keep, terms):
    vmem = pl.BlockSpec(memory_space=pltpu.VMEM)
    operands = [pltpu.with_memory_space_constraint(term, pltpu.VMEM) for term in terms]
    return pl.pallas_call(
        mean_kernel,
        out_shape=jax.ShapeDtypeStruct(terms[0].shape, jnp.bfloat16),
        in_specs=[vmem] * (1 + len(operands)),
        out_specs=pl.BlockSpec(memory_space=pl.ANY),
        scratch_shapes=[
            pltpu.VMEM(terms[0].shape, jnp.bfloat16),
            pltpu.SemaphoreType.DMA((2,)),
        ],
        compiler_params=pltpu.CompilerParams(vmem_limit_bytes=VMEM_LIMIT),
        name="mean_of_visits",
    )(keep, *operands)


def stage_kernel(lengths_ref, query_any, gain_any, cosine_any, sine_any, *refs):
    query_ref, gain_ref, cosine_ref, sine_ref, keep_ref, token_ref, *biases = refs[:-1]
    sems = refs[-1]
    parts = query_ref.shape[0]
    moves = [(gain_any, gain_ref), (cosine_any, cosine_ref), (sine_any, sine_ref)]
    strip = query_ref.shape[1] // STRIPS
    for part in range(parts):
        for number in range(STRIPS):
            place = pl.ds(number * strip, strip)
            moves.append((query_any.at[part, place], query_ref.at[part, place]))
    copies = [
        pltpu.make_async_copy(source, target, sems.at[number])
        for number, (source, target) in enumerate(moves)
    ]
    for copy in copies:
        copy.start()
    snap = lax.axis_index("snap")
    snaps = lax.axis_size("snap")
    rows = keep_ref.shape[0]
    token_ref[...] = jnp.zeros(token_ref.shape, token_ref.dtype)
    row = lax.broadcasted_iota(jnp.int32, keep_ref.shape, 0)
    keep_ref[...] = jnp.where(row < lengths_ref[snap], 1.0, 0.0)
    row = lax.broadcasted_iota(jnp.int32, (rows, rows), 1)
    key = lax.broadcasted_iota(jnp.int32, (rows, rows), 0)
    for visit, bias_ref in enumerate(biases):
        length = lengths_ref[visiting_block(snap, snaps, visit)]
        bias_ref[...] = jnp.where((key <= row) & (key < length), 0.0, -1e30)
    for copy in copies:
        copy.wait()


def staged(lengths, query, gain, cosine, sine, rows):
    hbm = pl.BlockSpec(memory_space=pltpu.HBM)
    vmem = pl.BlockSpec(memory_space=pltpu.VMEM)
    held = [(array.shape, array.dtype) for array in (query, gain, cosine, sine)]
    held += [((rows, LANES), jnp.float32)]
    biases = [((rows, rows), jnp.float32)] * VISITS
    return pl.pallas_call(
        stage_kernel,
        out_shape=[
            *(pltpu.VMEM(*each) for each in held),
            jax.ShapeDtypeStruct((8, LANES), jnp.float32),
            *(pltpu.VMEM(*each) for each in biases),
        ],
        in_specs=[pl.BlockSpec(memory_space=pltpu.SMEM)] + [hbm] * 4,
        out_specs=[vmem] * (len(held) + 1 + len(biases)),
        scratch_shapes=[pltpu.SemaphoreType.DMA((3 + STRIPS * query.shape[0],))],
        compiler_params=pltpu.CompilerParams(vmem_limit_bytes=VMEM_LIMIT),
        name="stage_weights",
    )(
        lengths,
        *(
            pltpu.with_memory_space_constraint(array, pltpu.HBM)
            for array in (query, gain, cosine, sine)
        ),
    )


def head_of(rank, heads_here):
    return (rank * heads_here) // (QHEADS // KVHEADS)


def cut_kernel(heads_here, keyval_ref, *out_refs):
    rank = lax.axis_index("tp")
    league = lax.axis_index("league")
    for bits, out_ref in enumerate(out_refs):
        rows, width = out_ref.shape
        head = head_of(lax.bitwise_xor(rank, jnp.int32(bits)), heads_here)
        columns = pl.ds(pl.multiple_of(head * width, LANES), width)
        if bits < 2:
            out_ref[...] = keyval_ref[:, columns]
        else:
            out_ref[...] = keyval_ref[pl.ds(pl.multiple_of(league * rows, 16), rows), columns]


def cut_keyval(keyval, heads_here, parts, leagues):
    features, width = keyval.shape[0], 2 * HD
    rows = [features // (1 if bits < 2 else leagues) for bits in range(parts)]
    vmem = pl.BlockSpec(memory_space=pltpu.VMEM)
    return pl.pallas_call(
        functools.partial(cut_kernel, heads_here),
        out_shape=[jax.ShapeDtypeStruct((count, width), keyval.dtype) for count in rows],
        in_specs=[vmem],
        out_specs=[vmem] * parts,
        compiler_params=pltpu.CompilerParams(vmem_limit_bytes=VMEM_LIMIT),
        name="cut_keyval",
    )(keyval)


def join_kernel(counts, *refs):
    passed = (len(refs) - 2 - sum(counts)) // 2
    pieces, refs = refs[: sum(counts)], refs[sum(counts) :]
    sources, out_ref, targets, sems = (
        refs[:passed],
        refs[passed],
        refs[passed + 1 : -1],
        refs[-1],
    )
    rank = lax.axis_index("tp")
    league = lax.axis_index("league")
    moves = []
    for bits, count in enumerate(counts):
        owner = lax.bitwise_xor(rank, jnp.int32(bits))
        for by in range(count):
            piece = pieces[len(moves)]
            rows = piece.shape[0]
            source = lax.rem(league + (count - by), count)
            place = pl.ds(pl.multiple_of(source * rows, 16), rows)
            moves.append((piece, out_ref.at[owner, place]))
    moves += list(zip(sources, targets))
    copies = [
        pltpu.make_async_copy(source, target, sems.at[number])
        for number, (source, target) in enumerate(moves)
    ]
    for copy in copies:
        copy.start()
    for copy in copies:
        copy.wait()


def join_keyval(groups, passed):
    any_space = pl.BlockSpec(memory_space=pl.ANY)
    pieces = [piece for group in groups for piece in group]
    features, width = pieces[0].shape
    keyval, *held = pl.pallas_call(
        functools.partial(join_kernel, [len(group) for group in groups]),
        out_shape=[
            pltpu.VMEM((len(groups), features, width), pieces[0].dtype),
            *(pltpu.VMEM(array.shape, array.dtype) for array in passed),
        ],
        in_specs=[any_space] * (len(pieces) + len(passed)),
        out_specs=[pl.BlockSpec(memory_space=pltpu.VMEM)] * (1 + len(passed)),
        scratch_shapes=[pltpu.SemaphoreType.DMA((len(pieces) + len(passed),))],
        compiler_params=pltpu.CompilerParams(vmem_limit_bytes=VMEM_LIMIT),
        name="join_keyval",
    )(*pieces, *passed)
    return keyval, held


def kept_order(array, *earlier):
    return lax.optimization_barrier((array, *earlier))[0]


def on_device(block_states, lengths, norm_gain, query_weight, keyval_weight):
    snaps = lax.axis_size("snap")
    parts = lax.axis_size("tp")
    leagues = lax.axis_size("league")
    own = block_states[0]
    rows, features = own.shape
    query = query_weight[0].reshape(parts, features, query_weight.shape[2])
    heads_here = query.shape[2] // HD
    cosine, sine = rope_tables(rows)

    def moved(block, visit):
        return lax.ppermute(block, "snap", visit_pairs(snaps, visit))

    def sent_home(visit, array):
        return lax.ppermute(array, "snap", visit_pairs(snaps, visit, back=True))

    if snaps == VISITS:
        block_2 = moved(own, 2)
        block_1 = moved(own, 1)
        block_3 = moved(block_2, 1)
    else:
        block_1 = moved(own, 1)
        block_2 = moved(block_1, 1)
        block_3 = moved(block_2, 1)

    query_held, gain_held, cosine_held, sine_held, keep, token, *biases = staged(
        lengths, query, norm_gain, cosine, sine, rows
    )

    columns = cut_keyval(keyval_weight[0], heads_here, parts, leagues)
    groups = [[columns[0]], [swapped(columns[1], 1)]]
    arrived = [swapped(columns[bits], bits) for bits in range(2, parts)]
    for piece in arrived:
        by_league = [kept_order(piece, token, block_1, block_2)]
        for _ in range(1, leagues):
            by_league.append(
                lax.ppermute(
                    by_league[-1], "league", [(i, (i + 1) % leagues) for i in range(leagues)]
                )
            )
        groups.append(by_league)

    def over_chips(block):
        return [block] + [swapped(block, bits) for bits in range(2, parts, 2)]

    pairs_of_cores = [[i, i + 1] for i in range(0, parts, 2)]

    def over_cores(shards, *earlier, apart=False):
        own_shard, *chips = shards
        gathered = [own_shard, swapped(own_shard, 1)]
        for shard in chips:
            shard = kept_order(shard, *earlier)
            if apart:
                gathered += [shard, swapped(shard, 1)]
            else:
                gathered.append(
                    lax.all_gather(shard, "tp", axis=0, tiled=True, axis_index_groups=pairs_of_cores)
                )
        return gathered

    shards_2 = over_chips(kept_order(block_2, token, *arrived))
    shards_3 = over_chips(kept_order(block_3, *shards_2[1:]))
    keyval, held = join_keyval(groups, shards_2[1:])

    def scored(visit, shards):
        return visit_context(
            visit, shards, gain_held, query_held, keyval, cosine_held, sine_held, biases[visit]
        )

    context_2 = scored(2, over_cores([shards_2[0], *held], block_1, apart=True))
    home_2 = sent_home(2, context_2)
    shards_1 = over_chips(kept_order(block_1, context_2))
    gathered_3 = over_cores(shards_3, context_2)
    shards_0 = over_chips(kept_order(own, gathered_3[-1], *shards_1[1:]))
    context_3 = scored(3, gathered_3)
    home_3 = sent_home(3, context_3)
    context_1 = scored(1, over_cores(shards_1, context_3))
    home_1 = sent_home(1, context_1)
    context_0 = scored(0, over_cores(shards_0, context_1))
    return mean_of(keep, [context_0, home_2, home_3, home_1])[None]


def solution(mesh):
    placed = (
        P(("league", "snap"), None, "tp"),
        P("league"),
        P("snap", None),
        P("snap", None, "tp"),
        P("snap", "tp", None),
    )
    return jax.shard_map(
        on_device,
        mesh=mesh,
        in_specs=placed,
        out_specs=P(("league", "snap"), None, "tp"),
        check_vma=False,
    )
```

```python
import functools

import jax
import jax.numpy as jnp
import numpy as np
from jax import lax
from jax.experimental import pallas as pl
from jax.experimental.pallas import tpu as pltpu
from jax.sharding import PartitionSpec as P

QHEADS = 64
KVHEADS = 4
HD = 64
VISITS = 4
LANES = 128
STRIPS = 4
VMEM_LIMIT = 16 * 1024 * 1024

EPSILON = 1e-05
ROPE_BASE = 500000.0
LOG2E = 1.4426950408889634


def visit_pairs(snaps, visit, back=False):
    if snaps == VISITS:
        return [(i, i ^ visit) for i in range(snaps)]
    return [(i, (i + (-visit if back else visit)) % snaps) for i in range(snaps)]


def visiting_block(snap, snaps, visit):
    if snaps == VISITS:
        return lax.bitwise_xor(snap, jnp.int32(visit))
    return lax.rem(snap + (snaps - visit), snaps)


def swapped(array, with_bits):
    count = lax.axis_size("tp")
    return lax.ppermute(array, "tp", [(i, i ^ with_bits) for i in range(count)])


def rope_tables(row_count):
    half = HD // 2
    positions = np.arange(row_count, dtype=np.float32)[:, None]
    frequency = np.float32(ROPE_BASE) ** (-np.arange(half, dtype=np.float32) * np.float32(2.0 / HD))
    angles = positions * frequency[None, :].astype(np.float32)
    cosine, sine = np.cos(angles), np.sin(angles)
    repeats = LANES // HD
    return (
        jnp.asarray(np.concatenate([cosine, cosine] * repeats, axis=1)),
        jnp.asarray(np.concatenate([-sine, sine] * repeats, axis=1)),
    )


def rotated(pair, cosine, signed_sine, in_first_half):
    half = HD // 2
    partner = jnp.where(
        in_first_half, pltpu.roll(pair, LANES - half, 1), pltpu.roll(pair, half, 1)
    )
    return pair * cosine + partner * signed_sine


def visit_kernel(parts, held, *refs):
    (own, beside, *chips), refs = refs[:held], refs[held:]
    gain_ref, query_ref, keyval_ref, cosine_ref, sine_ref, bias_ref = refs[:6]
    out_ref, total_ref, queries_ref, scores_ref, probabilities_ref = refs[6:]
    rows, features = own.shape
    columns = query_ref.shape[2]
    width = parts * features
    step = 2 * LANES
    pairs = columns // LANES
    rank = lax.axis_index("tp")

    shards = [(own, 0, rank), (beside, 0, lax.bitwise_xor(rank, jnp.int32(1)))]
    if held == parts:
        for bits, shard in enumerate(chips, 2):
            shards.append((shard, 0, lax.bitwise_xor(rank, jnp.int32(bits))))
    else:
        for number, chip in enumerate(chips):
            first = lax.bitwise_xor(rank, jnp.int32(2 * (number + 1)))
            first = first - lax.rem(first, 2)
            shards += [(chip, 0, first), (chip, rows, first + 1)]

    squares = jnp.zeros((rows, 1), jnp.float32)
    for shard, start, _ in shards:
        values = shard[start : start + rows].astype(jnp.float32)
        squares += jnp.sum(values * values, axis=1, keepdims=True)
    scale = lax.rsqrt(squares / width + EPSILON)
    keyval = jnp.zeros((rows, keyval_ref.shape[2]), jnp.float32)

    def multiply(normed, owner, first):
        for start in range(0, columns, step):
            place = slice(start, start + step)
            product = jnp.dot(
                normed, query_ref[owner, :, place], preferred_element_type=jnp.float32
            )
            if first:
                total_ref[:, place] = product
            else:
                total_ref[:, place] += product
        return jnp.dot(normed, keyval_ref[owner], preferred_element_type=jnp.float32)

    for number, (shard, start, owner) in enumerate(shards):
        values = shard[start : start + rows].astype(jnp.float32)
        gain = gain_ref[:, pl.ds(pl.multiple_of(owner * features, LANES), features)]
        normed = (values * scale * gain).astype(jnp.bfloat16)
        keyval += multiply(normed, owner, number == 0)

    cosine, sine = cosine_ref[...], sine_ref[...]
    lane = lax.broadcasted_iota(jnp.int32, (rows, LANES), 1)
    in_first_half = lax.rem(lane, HD) < HD // 2
    in_first_head = lane < HD
    keyval = keyval.astype(jnp.bfloat16).astype(jnp.float32)
    keys = jnp.where(in_first_head, rotated(keyval, cosine, sine, in_first_half), 0.0)
    keys = jnp.concatenate([keys, pltpu.roll(keys, HD, 1)], axis=0).astype(jnp.bfloat16)
    values = jnp.where(in_first_head, 0.0, keyval)
    values = jnp.concatenate([pltpu.roll(values, HD, 1), values], axis=0).T.astype(jnp.bfloat16)

    for pair in range(pairs):
        place = slice(pair * LANES, (pair + 1) * LANES)
        queries_ref[:, place] = rotated(total_ref[:, place], cosine, sine, in_first_half).astype(
            jnp.bfloat16
        )
    for pair in range(pairs):
        scores_ref[pair] = lax.dot_general(
            keys,
            queries_ref[:, pair * LANES : (pair + 1) * LANES],
            (((1,), (1,)), ((), ())),
            preferred_element_type=jnp.float32,
        )
    for pair in range(pairs):
        for head in range(2):
            place = slice(head * rows, (head + 1) * rows)
            mine = scores_ref[pair, place] + bias_ref[...]
            top = jnp.max(mine, axis=0, keepdims=True)
            weights = jnp.exp2((mine - top) * (LOG2E * HD**-0.5))
            whole = jnp.sum(weights, axis=0, keepdims=True)
            probabilities_ref[pair, place] = (weights * (1.0 / whole)).astype(jnp.bfloat16)
    for pair in range(pairs):
        context = jnp.dot(values, probabilities_ref[pair], preferred_element_type=jnp.float32)
        out_ref[:, pair * LANES : (pair + 1) * LANES] = context.T.astype(jnp.bfloat16)


def visit_context(visit, shards, gain, query, keyval, cosine, sine, bias):
    parts, features, columns = query.shape
    rows = shards[0].shape[0]
    vmem = pl.BlockSpec(memory_space=pltpu.VMEM)
    operands = (*shards, gain, query, keyval, cosine, sine, bias)
    scores = (columns // LANES, 2 * rows, rows)
    return pl.pallas_call(
        functools.partial(visit_kernel, parts, len(shards)),
        out_shape=pltpu.VMEM((rows, columns), jnp.bfloat16),
        in_specs=[vmem] * len(operands),
        out_specs=vmem,
        scratch_shapes=[
            pltpu.VMEM((rows, columns), jnp.float32),
            pltpu.VMEM((rows, columns), jnp.bfloat16),
            pltpu.VMEM(scores, jnp.float32),
            pltpu.VMEM(scores, jnp.bfloat16),
        ],
        compiler_params=pltpu.CompilerParams(vmem_limit_bytes=VMEM_LIMIT),
        cost_estimate=pl.CostEstimate(flops=1, bytes_accessed=1, transcendentals=0),
        name=f"visit_{visit}",
    )(*operands)


def mean_kernel(keep_ref, *refs):
    terms, (out_any, out_ref, sems) = refs[:-3], refs[-3:]
    rows, _ = out_ref.shape
    strips = 2
    strip = rows // strips
    leaving = []
    for number in range(strips):
        place = pl.ds(number * strip, strip)
        total = terms[0][place].astype(jnp.float32)
        for term in terms[1:]:
            total += term[place].astype(jnp.float32)
        keep = keep_ref[place, :1] > 0.0
        out_ref[place] = jnp.where(keep, total / VISITS, 0.0).astype(jnp.bfloat16)
        leaving.append(
            pltpu.make_async_copy(out_ref.at[place], out_any.at[place], sems.at[number])
        )
        leaving[-1].start()
    for copy in leaving:
        copy.wait()


def early_kernel(*refs):
    terms, out_ref = refs[:-1], refs[-1]
    total = terms[0][...].astype(jnp.float32)
    for term in terms[1:]:
        total += term[...].astype(jnp.float32)
    out_ref[...] = total


def early_sum(terms):
    vmem = pl.BlockSpec(memory_space=pltpu.VMEM)
    operands = [pltpu.with_memory_space_constraint(term, pltpu.VMEM) for term in terms]
    return pl.pallas_call(
        early_kernel,
        out_shape=pltpu.VMEM(terms[0].shape, jnp.float32),
        in_specs=[vmem] * len(operands),
        out_specs=vmem,
        compiler_params=pltpu.CompilerParams(vmem_limit_bytes=VMEM_LIMIT),
        cost_estimate=pl.CostEstimate(flops=1, bytes_accessed=1, transcendentals=0),
        name="early_sum",
    )(*operands)


def mean_of(keep, terms):
    vmem = pl.BlockSpec(memory_space=pltpu.VMEM)
    operands = [pltpu.with_memory_space_constraint(term, pltpu.VMEM) for term in terms]
    return pl.pallas_call(
        mean_kernel,
        out_shape=jax.ShapeDtypeStruct(terms[0].shape, jnp.bfloat16),
        in_specs=[vmem] * (1 + len(operands)),
        out_specs=pl.BlockSpec(memory_space=pl.ANY),
        scratch_shapes=[
            pltpu.VMEM(terms[0].shape, jnp.bfloat16),
            pltpu.SemaphoreType.DMA((2,)),
        ],
        compiler_params=pltpu.CompilerParams(vmem_limit_bytes=VMEM_LIMIT),
        name="mean_of_visits",
    )(keep, *operands)


def stage_kernel(lengths_ref, query_any, gain_any, cosine_any, sine_any, *refs):
    query_ref, gain_ref, cosine_ref, sine_ref, keep_ref, token_ref, *biases = refs[:-1]
    sems = refs[-1]
    parts = query_ref.shape[0]
    moves = [(gain_any, gain_ref), (cosine_any, cosine_ref), (sine_any, sine_ref)]
    strip = query_ref.shape[1] // STRIPS
    for part in range(parts):
        for number in range(STRIPS):
            place = pl.ds(number * strip, strip)
            moves.append((query_any.at[part, place], query_ref.at[part, place]))
    copies = [
        pltpu.make_async_copy(source, target, sems.at[number])
        for number, (source, target) in enumerate(moves)
    ]
    for copy in copies:
        copy.start()
    snap = lax.axis_index("snap")
    snaps = lax.axis_size("snap")
    rows = keep_ref.shape[0]
    token_ref[...] = jnp.zeros(token_ref.shape, token_ref.dtype)
    row = lax.broadcasted_iota(jnp.int32, keep_ref.shape, 0)
    keep_ref[...] = jnp.where(row < lengths_ref[snap], 1.0, 0.0)
    row = lax.broadcasted_iota(jnp.int32, (rows, rows), 1)
    key = lax.broadcasted_iota(jnp.int32, (rows, rows), 0)
    for visit, bias_ref in enumerate(biases):
        length = lengths_ref[visiting_block(snap, snaps, visit)]
        bias_ref[...] = jnp.where((key <= row) & (key < length), 0.0, -1e30)
    for copy in copies:
        copy.wait()


def staged(lengths, query, gain, cosine, sine, rows):
    hbm = pl.BlockSpec(memory_space=pltpu.HBM)
    vmem = pl.BlockSpec(memory_space=pltpu.VMEM)
    held = [(array.shape, array.dtype) for array in (query, gain, cosine, sine)]
    held += [((rows, LANES), jnp.float32)]
    biases = [((rows, rows), jnp.float32)] * VISITS
    return pl.pallas_call(
        stage_kernel,
        out_shape=[
            *(pltpu.VMEM(*each) for each in held),
            jax.ShapeDtypeStruct((8, LANES), jnp.float32),
            *(pltpu.VMEM(*each) for each in biases),
        ],
        in_specs=[pl.BlockSpec(memory_space=pltpu.SMEM)] + [hbm] * 4,
        out_specs=[vmem] * (len(held) + 1 + len(biases)),
        scratch_shapes=[pltpu.SemaphoreType.DMA((3 + STRIPS * query.shape[0],))],
        compiler_params=pltpu.CompilerParams(vmem_limit_bytes=VMEM_LIMIT),
        name="stage_weights",
    )(
        lengths,
        *(
            pltpu.with_memory_space_constraint(array, pltpu.HBM)
            for array in (query, gain, cosine, sine)
        ),
    )


def head_of(rank, heads_here):
    return (rank * heads_here) // (QHEADS // KVHEADS)


def cut_kernel(heads_here, keyval_ref, *out_refs):
    rank = lax.axis_index("tp")
    league = lax.axis_index("league")
    for bits, out_ref in enumerate(out_refs):
        rows, width = out_ref.shape
        head = head_of(lax.bitwise_xor(rank, jnp.int32(bits)), heads_here)
        columns = pl.ds(pl.multiple_of(head * width, LANES), width)
        if bits < 2:
            out_ref[...] = keyval_ref[:, columns]
        else:
            out_ref[...] = keyval_ref[pl.ds(pl.multiple_of(league * rows, 16), rows), columns]


def cut_keyval(keyval, heads_here, parts, leagues):
    features, width = keyval.shape[0], 2 * HD
    rows = [features // (1 if bits < 2 else leagues) for bits in range(parts)]
    vmem = pl.BlockSpec(memory_space=pltpu.VMEM)
    return pl.pallas_call(
        functools.partial(cut_kernel, heads_here),
        out_shape=[jax.ShapeDtypeStruct((count, width), keyval.dtype) for count in rows],
        in_specs=[vmem],
        out_specs=[vmem] * parts,
        compiler_params=pltpu.CompilerParams(vmem_limit_bytes=VMEM_LIMIT),
        name="cut_keyval",
    )(keyval)


def join_kernel(counts, *refs):
    passed = (len(refs) - 2 - sum(counts)) // 2
    pieces, refs = refs[: sum(counts)], refs[sum(counts) :]
    sources, out_ref, targets, sems = (
        refs[:passed],
        refs[passed],
        refs[passed + 1 : -1],
        refs[-1],
    )
    rank = lax.axis_index("tp")
    league = lax.axis_index("league")
    moves = []
    for bits, count in enumerate(counts):
        owner = lax.bitwise_xor(rank, jnp.int32(bits))
        for by in range(count):
            piece = pieces[len(moves)]
            rows = piece.shape[0]
            source = lax.rem(league + (count - by), count)
            place = pl.ds(pl.multiple_of(source * rows, 16), rows)
            moves.append((piece, out_ref.at[owner, place]))
    moves += list(zip(sources, targets))
    copies = [
        pltpu.make_async_copy(source, target, sems.at[number])
        for number, (source, target) in enumerate(moves)
    ]
    for copy in copies:
        copy.start()
    for copy in copies:
        copy.wait()


def join_keyval(groups, passed):
    any_space = pl.BlockSpec(memory_space=pl.ANY)
    pieces = [piece for group in groups for piece in group]
    features, width = pieces[0].shape
    keyval, *held = pl.pallas_call(
        functools.partial(join_kernel, [len(group) for group in groups]),
        out_shape=[
            pltpu.VMEM((len(groups), features, width), pieces[0].dtype),
            *(pltpu.VMEM(array.shape, array.dtype) for array in passed),
        ],
        in_specs=[any_space] * (len(pieces) + len(passed)),
        out_specs=[pl.BlockSpec(memory_space=pltpu.VMEM)] * (1 + len(passed)),
        scratch_shapes=[pltpu.SemaphoreType.DMA((len(pieces) + len(passed),))],
        compiler_params=pltpu.CompilerParams(vmem_limit_bytes=VMEM_LIMIT),
        name="join_keyval",
    )(*pieces, *passed)
    return keyval, held


def kept_order(array, *earlier):
    return lax.optimization_barrier((array, *earlier))[0]


def on_device(block_states, lengths, norm_gain, query_weight, keyval_weight):
    snaps = lax.axis_size("snap")
    parts = lax.axis_size("tp")
    leagues = lax.axis_size("league")
    own = block_states[0]
    rows, features = own.shape
    query = query_weight[0].reshape(parts, features, query_weight.shape[2])
    heads_here = query.shape[2] // HD
    cosine, sine = rope_tables(rows)

    def moved(block, visit):
        return lax.ppermute(block, "snap", visit_pairs(snaps, visit))

    def sent_home(visit, array):
        return lax.ppermute(array, "snap", visit_pairs(snaps, visit, back=True))

    if snaps == VISITS:
        block_2 = moved(own, 2)
        block_1 = moved(own, 1)
        block_3 = moved(block_2, 1)
    else:
        block_1 = moved(own, 1)
        block_2 = moved(block_1, 1)
        block_3 = moved(block_2, 1)

    query_held, gain_held, cosine_held, sine_held, keep, token, *biases = staged(
        lengths, query, norm_gain, cosine, sine, rows
    )

    columns = cut_keyval(keyval_weight[0], heads_here, parts, leagues)
    groups = [[columns[0]], [swapped(columns[1], 1)]]
    arrived = [swapped(columns[bits], bits) for bits in range(2, parts)]
    for piece in arrived:
        by_league = [kept_order(piece, token, block_1, block_2)]
        for _ in range(1, leagues):
            by_league.append(
                lax.ppermute(
                    by_league[-1], "league", [(i, (i + 1) % leagues) for i in range(leagues)]
                )
            )
        groups.append(by_league)

    def over_chips(block):
        return [block] + [swapped(block, bits) for bits in range(2, parts, 2)]

    pairs_of_cores = [[i, i + 1] for i in range(0, parts, 2)]

    def over_cores(shards, *earlier, apart=False):
        own_shard, *chips = shards
        gathered = [own_shard, swapped(own_shard, 1)]
        for shard in chips:
            shard = kept_order(shard, *earlier)
            if apart:
                gathered += [shard, swapped(shard, 1)]
            else:
                gathered.append(
                    lax.all_gather(shard, "tp", axis=0, tiled=True, axis_index_groups=pairs_of_cores)
                )
        return gathered

    shards_2 = over_chips(kept_order(block_2, token, *arrived))
    shards_3 = over_chips(kept_order(block_3, *shards_2[1:]))
    keyval, held = join_keyval(groups, shards_2[1:])

    def scored(visit, shards):
        return visit_context(
            visit, shards, gain_held, query_held, keyval, cosine_held, sine_held, biases[visit]
        )

    context_2 = scored(2, over_cores([shards_2[0], *held], block_1, apart=True))
    home_2 = sent_home(2, context_2)
    shards_1 = over_chips(kept_order(block_1, context_2))
    gathered_3 = over_cores(shards_3, context_2)
    shards_0 = over_chips(kept_order(own, gathered_3[-1], *shards_1[1:]))
    context_3 = scored(3, gathered_3)
    home_3 = sent_home(3, context_3)
    context_1 = scored(1, over_cores(shards_1, context_3))
    home_1 = sent_home(1, context_1)
    context_0 = scored(0, over_cores(shards_0, context_1))
    return mean_of(keep, [home_1, early_sum([context_0, home_2, home_3])])[None]


def solution(mesh):
    placed = (
        P(("league", "snap"), None, "tp"),
        P("league"),
        P("snap", None),
        P("snap", None, "tp"),
        P("snap", "tp", None),
    )
    return jax.shard_map(
        on_device,
        mesh=mesh,
        in_specs=placed,
        out_specs=P(("league", "snap"), None, "tp"),
        check_vma=False,
    )
```
